32 devices in a mesh: pipe: 2 (over x), ctx: 4 (over y, core), dp: 4 (over z).
Axes of the slice: x: 2, y: 2, z: 4, core: 2. Of those that a mesh axis runs over, the one named last changes fastest.
Arguments:
- patches: bfloat16 [1, 4, 512, 1024], P(None, 'dp', 'ctx'), may hold values from -6 to 6
- lengths: int32 [1, 4], P(None, 'dp'), may hold values from 128 to 512, as said below
- norm_gain: float32 [2, 1024], P('pipe'), may hold values from 0.1 to 1.9
- norm_bias: float32 [2, 1024], P('pipe'), may hold values from -3 to 3
- w_qkv: bfloat16 [2, 1024, 3072], P('pipe', None, 'dp')
- w_out: bfloat16 [2, 1024, 1024], P('pipe'), may hold values from -0.1875 to 0.1875
- out_bias: float32 [2, 1024], P('pipe'), may hold values from -3 to 3
- scale_gain: float32 [2, 1024], P('pipe'), may hold values from 0.3 to 1.5
Outputs:
- section_outputs: bfloat16 [2, 1, 4, 512, 1024], P('pipe', None, 'dp', 'ctx')
The draws below stay inside these ranges and needn't reach their ends.
Inputs may be any that keep to these rules, and one draw needn't show every extreme that they name: `lengths`: every volume has at least 128 real tokens, and in every draw some volume fills all 512 slots.
All inputs are finite; a program needn't handle non-finite values.
Results may differ from the reference program's by a relative error of at most 0.017.
The reference program's roundings to bfloat16 on the way count: a program that leaves them out, or rounds other values in their place, can miss the bound.
Values may be sent and summed in bfloat16 or wider, within the bound.
A program may use at most 128 MiB of HBM per device.

```python
import math
import jax
import jax.numpy as jnp
from jax import lax

D = 1024
HEADS = 16
HEAD_DIM = 64
MICRO = 1
SEQ = 512
VOLUMES = 4
N_PIPE = 2


def draw_lengths(key, part):
    total_count = MICRO * VOLUMES
    drawn = jax.random.randint(key, (total_count,), SEQ // 4, SEQ + 1)
    chosen = jax.random.randint(jax.random.fold_in(key, 7), (), 0, total_count)
    drawn = jnp.where(jnp.arange(total_count) == chosen, SEQ, drawn)
    return drawn.reshape(MICRO, VOLUMES).astype(jnp.int32)


def draw_w_qkv(key, part):
    base_scale = math.sqrt(2.0 / D)
    first_key = jax.random.fold_in(key, 0)
    third_key = jax.random.fold_in(key, 2)
    fourth_key = jax.random.fold_in(key, 3)
    query_part = jax.random.normal(first_key, (N_PIPE, D, D), jnp.float32) * base_scale
    key_part = jax.random.normal(fourth_key, (N_PIPE, D, D), jnp.float32) * base_scale
    value_part = jax.random.normal(third_key, (N_PIPE, D, D), jnp.float32) * base_scale
    return jnp.concatenate([query_part, key_part, value_part], axis=-1).astype(jnp.bfloat16)


def block_levels(stream_key, dims, cuts, smallest, largest):
    level, own = 1.0, jax.random.fold_in(stream_key, 6)
    for axis_at, shards_of in cuts:
        steps = jnp.exp(jax.random.uniform(jax.random.fold_in(own, axis_at), (shards_of,), jnp.float32, smallest / len(cuts), largest / len(cuts)))
        level = level * jnp.repeat(steps, dims[axis_at] // shards_of).reshape([-1 if axis == axis_at else 1 for axis in range(len(dims))])
    return level


def normal_values(own_key, dims, deviation, reach, cuts=(), held_as=jnp.bfloat16):
    array = jax.random.normal(own_key, dims, jnp.float32) * deviation
    if len(cuts) > 0:
        array = block_levels(own_key, dims, cuts, -0.22, 0.18) * array
    return jnp.clip(array, min=-reach, max=reach).astype(held_as)


def setup_inputs(seed: int = 0) -> dict:
    streams_of = jax.random.split(jax.random.key(seed), 9)
    return {
        "patches": normal_values(streams_of[0], (MICRO, VOLUMES, SEQ, D), 1.0, 6.0, ((1, 4), (2, 4))),
        "lengths": draw_lengths(jax.random.fold_in(streams_of[8], 71), 0),
        "norm_gain": jnp.clip(1.0 + 0.18 * jax.random.normal(streams_of[2], (N_PIPE, D), jnp.float32), 0.1, 1.9),
        "norm_bias": normal_values(streams_of[3], (N_PIPE, D), 0.5, 3.0, ((0, 2),), jnp.float32),
        "w_qkv": draw_w_qkv(jax.random.fold_in(streams_of[8], 71), 0),
        "w_out": normal_values(streams_of[5], (N_PIPE, D, D), D ** -0.5, 0.1875, ((0, 2),)),
        "out_bias": normal_values(streams_of[6], (N_PIPE, D), 0.5, 3.0, ((0, 2),), jnp.float32),
        "scale_gain": jnp.clip(jnp.exp(math.log(1.5) - 1.60943787 * jax.random.uniform(streams_of[7], (N_PIPE, D), jnp.float32) ** block_levels(streams_of[7], (N_PIPE, D), ((0, 2),), -0.2, 0.2)), 0.3, 1.5),
    }


epsilon = 1e-06
masked_score = -1e+30

def normalize(hidden, gain, shift):
    values = hidden.astype(jnp.float32)
    row_mean = lax.optimization_barrier(jnp.mean(values, axis=-1, keepdims=True))
    centered = values - row_mean
    variance = lax.optimization_barrier(jnp.mean(centered * centered, axis=-1, keepdims=True))
    return (centered * lax.rsqrt(variance + epsilon) * gain + shift).astype(jnp.bfloat16)

def sublayer(hidden, length, gain, shift, qkv_weight, out_weight, out_shift, layer_scale):
    normed = normalize(hidden, gain, shift)
    projected = jnp.dot(normed, qkv_weight, preferred_element_type=jnp.float32).astype(jnp.bfloat16)
    projected = projected.reshape(SEQ, 3, HEADS, HEAD_DIM)
    queries = projected[:, 0].astype(jnp.float32)
    key_rows = projected[:, 1].astype(jnp.float32)
    value_rows = projected[:, 2].astype(jnp.float32)
    scores = jnp.einsum('qhd,khd->hqk', queries, key_rows) * HEAD_DIM ** (-0.5)
    valid = jnp.arange(SEQ, dtype=jnp.int32) < length
    scores = jnp.where(valid[None, None, :], scores, masked_score)
    top_score = lax.optimization_barrier(jnp.max(scores, axis=-1, keepdims=True))
    weights = jnp.where(valid[None, None, :], jnp.exp(scores - top_score), 0.0)
    totals = lax.optimization_barrier(jnp.sum(weights, axis=-1))
    rounded = lax.optimization_barrier(weights.astype(jnp.bfloat16)).astype(jnp.float32)
    context = jnp.einsum('hqk,khd->qhd', rounded, value_rows) / totals.T[:, :, None]
    context = context.astype(jnp.bfloat16).reshape(SEQ, D)
    mixed = jnp.dot(context, out_weight, preferred_element_type=jnp.float32) + out_shift
    return (hidden.astype(jnp.float32) + layer_scale * mixed).astype(jnp.bfloat16)

def reference(patches, lengths, norm_gain, norm_bias, w_qkv, w_out, out_bias, scale_gain):
    current = patches.reshape(MICRO * VOLUMES, SEQ, D)
    flat_lengths = lengths.reshape(MICRO * VOLUMES)
    collected = []
    for layer_index in range(N_PIPE):

        def run_volume(item, layer_index=layer_index):
            return sublayer(item[0], item[1], norm_gain[layer_index], norm_bias[layer_index], w_qkv[layer_index], w_out[layer_index], out_bias[layer_index], scale_gain[layer_index])
        current = lax.map(run_volume, (current, flat_lengths))
        collected.append(current.reshape(MICRO, VOLUMES, SEQ, D))
    return jnp.stack(collected)
```

```python
import functools
import math

import jax
import jax.numpy as jnp
from jax import lax
from jax.experimental import pallas as pl
from jax.experimental.pallas import tpu as pltpu
from jax.sharding import PartitionSpec as P

HEADS = 16


epsilon = 1e-06
masked_score = -1e30


def shifted(value, axis, by):
    count = lax.axis_size(axis)
    pairs = [(i, i + by) for i in range(count) if 0 <= i + by < count]
    return lax.ppermute(value, axis, pairs)


def normalize(hidden, gain, shift):
    values = hidden.astype(jnp.float32)
    row_mean = jnp.mean(values, axis=-1, keepdims=True)
    centered = values - row_mean
    variance = jnp.mean(centered * centered, axis=-1, keepdims=True)
    return (centered * lax.rsqrt(variance + epsilon) * gain + shift).astype(jnp.bfloat16)


def per_device(patches, lengths, norm_gain, norm_bias, w_qkv, w_out, out_bias, scale_gain):
    section_index = lax.axis_index("pipe")
    section_count = lax.axis_size("pipe")
    group_count = lax.axis_size("ctx")
    micro_count = patches.shape[0]
    tok_rows = patches.shape[2]
    width = patches.shape[3]
    head_count = HEADS
    head_width = width // head_count
    group_heads = head_count // group_count
    score_scale = head_width ** (-0.5)
    qkv_full = lax.all_gather(w_qkv[0], "dp", axis=1, tiled=True)
    out_full = w_out[0]
    gain = norm_gain[0]
    shift = norm_bias[0]
    out_shift = out_bias[0]
    layer_scale = scale_gain[0]
    turn_count = micro_count + section_count - 1
    received = jnp.zeros((tok_rows, width), jnp.bfloat16)
    results = jnp.zeros((micro_count, tok_rows, width), jnp.bfloat16)
    volume_lengths = lengths[:, 0]
    for turn_index in range(turn_count):
        fresh = patches[min(turn_index, micro_count - 1), 0]
        current = jnp.where(section_index == 0, fresh, received)
        offset_turn = turn_index - section_index
        slot_index = jnp.clip(offset_turn, 0, micro_count - 1)
        length = lax.dynamic_index_in_dim(volume_lengths, slot_index, keepdims=False)
        normed = normalize(current, gain, shift)
        run_projected = jnp.dot(normed, qkv_full, preferred_element_type=jnp.float32).astype(
            jnp.bfloat16
        )
        run_projected = run_projected.reshape(tok_rows, 3, head_count, head_width)
        split_heads = run_projected.reshape(tok_rows, 3, group_count, group_heads, head_width)
        block = lax.all_to_all(split_heads, "ctx", split_axis=2, concat_axis=0, tiled=True)
        queries = block[:, 0, 0]
        key_rows = block[:, 1, 0]
        value_rows = block[:, 2, 0]
        total_rows = key_rows.shape[0]
        local_heads = queries.shape[1]
        valid = jnp.arange(total_rows, dtype=jnp.int32) < length
        query_block = math.gcd(total_rows, 512)
        grouped = queries.reshape(total_rows // query_block, query_block, local_heads, head_width)

        def one_block(query_group):
            scores = (
                jnp.einsum(
                    "qhd,khd->hqk", query_group, key_rows, preferred_element_type=jnp.float32
                )
                * score_scale
            )
            scores = jnp.where(valid[None, None, :], scores, masked_score)
            top_score = jnp.max(scores, axis=-1, keepdims=True)
            weights = jnp.where(valid[None, None, :], jnp.exp(scores - top_score), 0.0)
            totals = jnp.sum(weights, axis=-1)
            context = (
                jnp.einsum(
                    "hqk,khd->qhd",
                    weights.astype(jnp.bfloat16),
                    value_rows,
                    preferred_element_type=jnp.float32,
                )
                / totals.T[:, :, None]
            )
            return context.astype(jnp.bfloat16)

        blocks_out = lax.map(one_block, grouped)
        per_head = blocks_out.reshape(total_rows, 1, local_heads, head_width)
        merged = lax.all_to_all(per_head, "ctx", split_axis=0, concat_axis=1, tiled=True)
        run_context = merged.reshape(tok_rows, head_count, head_width)
        run_context = run_context.reshape(tok_rows, width)
        mixed = jnp.dot(run_context, out_full, preferred_element_type=jnp.float32) + out_shift
        produced = (current.astype(jnp.float32) + layer_scale * mixed).astype(jnp.bfloat16)
        keep_it = (offset_turn >= 0) & (offset_turn < micro_count)
        previous = lax.dynamic_index_in_dim(results, slot_index, keepdims=False)
        results = lax.dynamic_update_index_in_dim(
            results, jnp.where(keep_it, produced, previous), slot_index, 0
        )
        if turn_index + 1 < turn_count:
            received = shifted(produced, "pipe", 1)
    return results[None, :, None]


MESH = pl.DeviceIdType.MESH
PARTS = 3
DEPTH_CHUNKS = 4
ROW_CHUNKS = 2


def fused_kernel(
    sizes,
    length_ref,
    patches_ref,
    gain_ref,
    shift_ref,
    w_ref,
    out_w_ref,
    out_shift_ref,
    layer_scale_ref,
    result_ref,
    hidden,
    normed,
    weights,
    out_w,
    mine,
    gathered,
    w_recv,
    w_up,
    w_down,
    t_send,
    t_recv,
    c_send,
    c_recv,
    p_send,
    p_recv,
    l_sem,
):
    rows, width, planes, group = sizes
    head_width = width // HEADS
    group_blocks = w_ref.shape[1] // group
    depth = width // DEPTH_CHUNKS
    piece = rows // ROW_CHUNKS
    pairs = group // 128
    pipe = lax.axis_index("pipe")
    ctx = lax.axis_index("ctx")
    plane = lax.axis_index("dp")
    core, side = ctx % 2, ctx // 2
    near = side * 2 + (1 - core)
    across = (1 - side) * 2 + core
    diagonal = 3 - ctx
    others = (near, across, diagonal)
    has_up = plane < planes - 1
    has_down = plane > 0

    out_w_copy = pltpu.make_async_copy(out_w_ref, out_w, l_sem.at[0])
    out_w_copy.start()

    def owner_of(part):
        return (part * 4 + ctx) // group_blocks

    def own_column(part):
        return pl.multiple_of(((part * 4 + ctx) % group_blocks) * group, group)

    for part in range(PARTS):
        own_copy = pltpu.make_async_copy(
            w_ref.at[:, pl.ds(own_column(part), group)], weights.at[part], l_sem.at[1 + part]
        )

        @pl.when(owner_of(part) == plane)
        def _(own_copy=own_copy):
            own_copy.start()

    barrier = pltpu.get_barrier_semaphore()
    pl.semaphore_signal(barrier, inc=1, device_id={"pipe": 1 - pipe}, device_id_type=MESH)
    for other in others:
        pl.semaphore_signal(barrier, inc=1, device_id={"ctx": other}, device_id_type=MESH)

    @pl.when(has_up)
    def _():
        pl.semaphore_signal(barrier, inc=1, device_id={"dp": plane + 1}, device_id_type=MESH)

    @pl.when(has_down)
    def _():
        pl.semaphore_signal(barrier, inc=1, device_id={"dp": plane - 1}, device_id_type=MESH)

    def normalize_piece(at):
        span = pl.ds(at * piece, piece)
        normed[ctx, span, :] = normalize(hidden[span, :], gain_ref[...], shift_ref[...])

    @pl.when(pipe == 0)
    def _():
        hidden[...] = patches_ref[...]
        for at in range(ROW_CHUNKS):
            normalize_piece(at)

    pl.semaphore_wait(barrier, 4 + has_up.astype(jnp.int32) + has_down.astype(jnp.int32))

    def w_copy(part, at, own, up):
        span = pl.ds(at * depth, depth)
        there = weights.at[part, span, :]
        here = w_ref.at[span, pl.ds(own_column(part), group)] if own else there
        return pltpu.make_async_remote_copy(
            src_ref=here,
            dst_ref=there,
            send_sem=(w_up if up else w_down).at[part, at],
            recv_sem=w_recv.at[part, at],
            device_id={"dp": plane + 1 if up else plane - 1},
            device_id_type=MESH,
        )

    for at in range(DEPTH_CHUNKS):
        for part in range(PARTS):
            is_own = owner_of(part) == plane

            @pl.when(is_own & has_up)
            def _(part=part, at=at):
                w_copy(part, at, True, True).start()

            @pl.when(is_own & has_down)
            def _(part=part, at=at):
                w_copy(part, at, True, False).start()

    def t_copy(which, at):
        whose = across if which == 2 else ctx
        block = normed.at[whose, pl.ds(at * piece, piece), :]
        return pltpu.make_async_remote_copy(
            src_ref=block,
            dst_ref=block,
            send_sem=t_send.at[which, at],
            recv_sem=t_recv.at[which, at],
            device_id={"ctx": across if which == 1 else near},
            device_id_type=MESH,
        )

    def send_piece(at):
        t_copy(1, at).start()
        t_copy(0, at).start()

    def pass_pieces():
        for at in range(ROW_CHUNKS):
            t_copy(1, at).wait_recv()
            t_copy(2, at).start()

    @pl.when(pipe == 0)
    def _():
        for at in range(ROW_CHUNKS):
            send_piece(at)

    for at in range(DEPTH_CHUNKS):
        for part in range(PARTS):
            owner = owner_of(part)

            @pl.when(owner != plane)
            def _(part=part, at=at):
                w_copy(part, at, False, True).wait_recv()

            @pl.when((owner < plane) & has_up)
            def _(part=part, at=at):
                w_copy(part, at, False, True).start()

            @pl.when((owner > plane) & has_down)
            def _(part=part, at=at):
                w_copy(part, at, False, False).start()

        if at == DEPTH_CHUNKS // 2:

            @pl.when(pipe == 0)
            def _():
                pass_pieces()

    def p_copy(at):
        block = hidden.at[pl.ds(at * piece, piece), :]
        return pltpu.make_async_remote_copy(
            src_ref=block,
            dst_ref=block,
            send_sem=p_send.at[at],
            recv_sem=p_recv.at[at],
            device_id={"pipe": 1 - pipe},
            device_id_type=MESH,
        )

    for part in range(PARTS):
        own_copy = pltpu.make_async_copy(
            w_ref.at[:, pl.ds(own_column(part), group)], weights.at[part], l_sem.at[1 + part]
        )

        @pl.when(owner_of(part) == plane)
        def _(own_copy=own_copy):
            own_copy.wait()

    @pl.when(pipe == 1)
    def _():
        for at in range(ROW_CHUNKS):
            p_copy(at).wait_recv()
            normalize_piece(at)
            send_piece(at)
        pass_pieces()

    for at in range(ROW_CHUNKS):
        t_copy(0, at).wait_recv()
        t_copy(2, at).wait_recv()

    total = 4 * rows
    tokens = normed[...].reshape(total, width)

    def project(part):
        return jnp.dot(tokens, weights[part], preferred_element_type=jnp.float32)

    queries = (project(0).astype(jnp.bfloat16) * jnp.bfloat16(head_width**-0.5)).astype(
        jnp.bfloat16
    )
    key_rows = project(1).astype(jnp.bfloat16)
    value_columns = project(2).T.astype(jnp.bfloat16)
    key_bias = jnp.where(
        lax.broadcasted_iota(jnp.int32, (total, 1), 0) < length_ref[0, 0], 0.0, masked_score
    )
    lane_head = lax.broadcasted_iota(jnp.int32, (total, 128), 1) // head_width

    def c_copy(other, which, pair):
        lanes = pl.ds(pair * 128, 128)
        return pltpu.make_async_remote_copy(
            src_ref=mine.at[pl.ds(pl.multiple_of(other * rows, rows), rows), lanes],
            dst_ref=gathered.at[ctx, :, lanes],
            send_sem=c_send.at[which, pair],
            recv_sem=c_recv.at[which, pair],
            device_id={"ctx": other},
            device_id_type=MESH,
        )

    per_pair = 128 // head_width
    for pair in range(pairs):
        pair_queries = queries[:, pair * 128 : (pair + 1) * 128]
        pair_keys = key_rows[:, pair * 128 : (pair + 1) * 128]
        columns = []
        for head in range(per_pair):
            head_queries = jnp.where(lane_head == head, pair_queries, jnp.bfloat16(0))
            scores = lax.dot_general(
                pair_keys,
                head_queries,
                (((1,), (1,)), ((), ())),
                preferred_element_type=jnp.float32,
            )
            scores = scores + key_bias
            top = jnp.max(scores, axis=0, keepdims=True)
            exps = jnp.exp(scores - top)
            totals = jnp.sum(exps, axis=0, keepdims=True)
            first = (pair * per_pair + head) * head_width
            part_sum = jnp.dot(
                value_columns[first : first + head_width, :],
                exps.astype(jnp.bfloat16),
                preferred_element_type=jnp.float32,
            )
            columns.append(part_sum / totals)
        context = jnp.concatenate(columns, axis=0).T.astype(jnp.bfloat16)
        mine[:, pair * 128 : (pair + 1) * 128] = context
        for which, other in ((1, across), (2, diagonal), (0, near)):
            c_copy(other, which, pair).start()

    own_rows = pl.ds(pl.multiple_of(ctx * rows, rows), rows)
    out_w_copy.wait()

    def out_part(block, whose):
        span = pl.ds(pl.multiple_of(whose * group, group), group)
        return jnp.dot(block, out_w[span, :], preferred_element_type=jnp.float32)

    mixed = out_part(mine[own_rows, :], ctx)
    for which, other in enumerate(others):
        for pair in range(pairs):
            c_copy(other, which, pair).wait_recv()
        mixed = mixed + out_part(gathered[other], other)
    mixed = mixed + out_shift_ref[...]
    produced = (
        hidden[...].astype(jnp.float32) + layer_scale_ref[...] * mixed
    ).astype(jnp.bfloat16)
    result_ref[...] = produced

    @pl.when(pipe == 0)
    def _():
        hidden[...] = produced
        for at in range(ROW_CHUNKS):
            p_copy(at).start()

    for at in range(DEPTH_CHUNKS):
        for part in range(PARTS):
            owner = owner_of(part)

            @pl.when((owner <= plane) & has_up)
            def _(part=part, at=at):
                w_copy(part, at, False, True).wait_send()

            @pl.when((owner >= plane) & has_down)
            def _(part=part, at=at):
                w_copy(part, at, False, False).wait_send()

    for at in range(ROW_CHUNKS):
        for which in range(3):
            t_copy(which, at).wait_send()
    for pair in range(pairs):
        for which, other in enumerate(others):
            c_copy(other, which, pair).wait_send()

    @pl.when(pipe == 0)
    def _():
        for at in range(ROW_CHUNKS):
            p_copy(at).wait_send()


def fused_device(
    mesh, patches, lengths, norm_gain, norm_bias, w_qkv, w_out, out_bias, scale_gain
):
    planes, groups = mesh.shape["dp"], mesh.shape["ctx"]
    micro_count, _, rows, width = patches.shape
    group = width // groups
    fits = (
        micro_count == 1
        and mesh.shape["pipe"] == 2
        and groups == 4
        and group % 128 == 0
        and 128 % (width // HEADS) == 0
        and w_qkv.shape[2] % group == 0
        and rows % (16 * ROW_CHUNKS) == 0
        and rows <= 128
    )
    if not fits:
        return per_device(
            patches, lengths, norm_gain, norm_bias, w_qkv, w_out, out_bias, scale_gain
        )
    bf16 = jnp.bfloat16
    pairs = group // 128
    vmem = pl.BlockSpec(memory_space=pltpu.VMEM)
    hbm = pl.BlockSpec(memory_space=pl.ANY)
    dma = pltpu.SemaphoreType.DMA
    result = pl.pallas_call(
        functools.partial(fused_kernel, (rows, width, planes, group)),
        out_shape=jax.ShapeDtypeStruct((rows, width), bf16),
        in_specs=[
            pl.BlockSpec(memory_space=pltpu.SMEM),
            vmem,
            vmem,
            vmem,
            hbm,
            hbm,
            vmem,
            vmem,
        ],
        out_specs=vmem,
        scratch_shapes=[
            pltpu.VMEM((rows, width), bf16),
            pltpu.VMEM((groups, rows, width), bf16),
            pltpu.VMEM((PARTS, width, group), bf16),
            pltpu.VMEM((width, width), bf16),
            pltpu.VMEM((groups * rows, group), bf16),
            pltpu.VMEM((groups, rows, group), bf16),
            dma((PARTS, DEPTH_CHUNKS)),
            dma((PARTS, DEPTH_CHUNKS)),
            dma((PARTS, DEPTH_CHUNKS)),
            dma((3, ROW_CHUNKS)),
            dma((3, ROW_CHUNKS)),
            dma((3, pairs)),
            dma((3, pairs)),
            dma((ROW_CHUNKS,)),
            dma((ROW_CHUNKS,)),
            dma((4,)),
        ],
        compiler_params=pltpu.CompilerParams(
            collective_id=0, has_side_effects=True, vmem_limit_bytes=48 * 1024 * 1024
        ),
    )(
        lengths,
        patches[0, 0],
        norm_gain,
        norm_bias,
        w_qkv[0],
        w_out[0],
        out_bias,
        scale_gain,
    )
    return result[None, None, None]


def solution(mesh):
    in_specs = (
        P(None, "dp", "ctx", None),
        P(None, "dp"),
        P("pipe", None),
        P("pipe", None),
        P("pipe", None, "dp"),
        P("pipe", None, None),
        P("pipe", None),
        P("pipe", None),
    )
    out_specs = P("pipe", None, "dp", "ctx", None)
    body = functools.partial(fused_device, mesh)
    return jax.shard_map(
        body, mesh=mesh, in_specs=in_specs, out_specs=out_specs, check_vma=False
    )
```

```python
import functools
import math

import jax
import jax.numpy as jnp
from jax import lax
from jax.experimental import pallas as pl
from jax.experimental.pallas import tpu as pltpu
from jax.sharding import PartitionSpec as P

HEADS = 16


epsilon = 1e-06
masked_score = -1e30


def shifted(value, axis, by):
    count = lax.axis_size(axis)
    pairs = [(i, i + by) for i in range(count) if 0 <= i + by < count]
    return lax.ppermute(value, axis, pairs)


def normalize(hidden, gain, shift):
    values = hidden.astype(jnp.float32)
    row_mean = jnp.mean(values, axis=-1, keepdims=True)
    centered = values - row_mean
    variance = jnp.mean(centered * centered, axis=-1, keepdims=True)
    return (centered * lax.rsqrt(variance + epsilon) * gain + shift).astype(jnp.bfloat16)


def per_device(patches, lengths, norm_gain, norm_bias, w_qkv, w_out, out_bias, scale_gain):
    section_index = lax.axis_index("pipe")
    section_count = lax.axis_size("pipe")
    group_count = lax.axis_size("ctx")
    micro_count = patches.shape[0]
    tok_rows = patches.shape[2]
    width = patches.shape[3]
    head_count = HEADS
    head_width = width // head_count
    group_heads = head_count // group_count
    score_scale = head_width ** (-0.5)
    qkv_full = lax.all_gather(w_qkv[0], "dp", axis=1, tiled=True)
    out_full = w_out[0]
    gain = norm_gain[0]
    shift = norm_bias[0]
    out_shift = out_bias[0]
    layer_scale = scale_gain[0]
    turn_count = micro_count + section_count - 1
    received = jnp.zeros((tok_rows, width), jnp.bfloat16)
    results = jnp.zeros((micro_count, tok_rows, width), jnp.bfloat16)
    volume_lengths = lengths[:, 0]
    for turn_index in range(turn_count):
        fresh = patches[min(turn_index, micro_count - 1), 0]
        current = jnp.where(section_index == 0, fresh, received)
        offset_turn = turn_index - section_index
        slot_index = jnp.clip(offset_turn, 0, micro_count - 1)
        length = lax.dynamic_index_in_dim(volume_lengths, slot_index, keepdims=False)
        normed = normalize(current, gain, shift)
        run_projected = jnp.dot(normed, qkv_full, preferred_element_type=jnp.float32).astype(
            jnp.bfloat16
        )
        run_projected = run_projected.reshape(tok_rows, 3, head_count, head_width)
        split_heads = run_projected.reshape(tok_rows, 3, group_count, group_heads, head_width)
        block = lax.all_to_all(split_heads, "ctx", split_axis=2, concat_axis=0, tiled=True)
        queries = block[:, 0, 0]
        key_rows = block[:, 1, 0]
        value_rows = block[:, 2, 0]
        total_rows = key_rows.shape[0]
        local_heads = queries.shape[1]
        valid = jnp.arange(total_rows, dtype=jnp.int32) < length
        query_block = math.gcd(total_rows, 512)
        grouped = queries.reshape(total_rows // query_block, query_block, local_heads, head_width)

        def one_block(query_group):
            scores = (
                jnp.einsum(
                    "qhd,khd->hqk", query_group, key_rows, preferred_element_type=jnp.float32
                )
                * score_scale
            )
            scores = jnp.where(valid[None, None, :], scores, masked_score)
            top_score = jnp.max(scores, axis=-1, keepdims=True)
            weights = jnp.where(valid[None, None, :], jnp.exp(scores - top_score), 0.0)
            totals = jnp.sum(weights, axis=-1)
            context = (
                jnp.einsum(
                    "hqk,khd->qhd",
                    weights.astype(jnp.bfloat16),
                    value_rows,
                    preferred_element_type=jnp.float32,
                )
                / totals.T[:, :, None]
            )
            return context.astype(jnp.bfloat16)

        blocks_out = lax.map(one_block, grouped)
        per_head = blocks_out.reshape(total_rows, 1, local_heads, head_width)
        merged = lax.all_to_all(per_head, "ctx", split_axis=0, concat_axis=1, tiled=True)
        run_context = merged.reshape(tok_rows, head_count, head_width)
        run_context = run_context.reshape(tok_rows, width)
        mixed = jnp.dot(run_context, out_full, preferred_element_type=jnp.float32) + out_shift
        produced = (current.astype(jnp.float32) + layer_scale * mixed).astype(jnp.bfloat16)
        keep_it = (offset_turn >= 0) & (offset_turn < micro_count)
        previous = lax.dynamic_index_in_dim(results, slot_index, keepdims=False)
        results = lax.dynamic_update_index_in_dim(
            results, jnp.where(keep_it, produced, previous), slot_index, 0
        )
        if turn_index + 1 < turn_count:
            received = shifted(produced, "pipe", 1)
    return results[None, :, None]


MESH = pl.DeviceIdType.MESH
PARTS = 3
DEPTH_CHUNKS = 8
SIDE_CHUNKS = 3
ROW_CHUNKS = 4


def fused_kernel(
    sizes,
    length_ref,
    patches_ref,
    gain_hbm,
    shift_hbm,
    w_ref,
    out_w_ref,
    out_shift_hbm,
    layer_scale_hbm,
    result_ref,
    gain_ref,
    shift_ref,
    out_shift_ref,
    layer_scale_ref,
    side_weights,
    hidden,
    normed,
    weights,
    out_w,
    mine,
    gathered,
    w_recv,
    w_up,
    w_down,
    t_send,
    t_recv,
    c_send,
    c_recv,
    p_send,
    p_recv,
    b_recv,
    b_up,
    b_down,
    b_cross,
    l_sem,
):
    rows, width, planes, group = sizes
    head_width = width // HEADS
    group_blocks = w_ref.shape[1] // group
    depth = width // DEPTH_CHUNKS
    piece = rows // ROW_CHUNKS
    pairs = group // 128
    pipe = lax.axis_index("pipe")
    ctx = lax.axis_index("ctx")
    plane = lax.axis_index("dp")
    core, side = ctx % 2, ctx // 2
    near = side * 2 + (1 - core)
    across = (1 - side) * 2 + core
    diagonal = 3 - ctx
    others = (near, across, diagonal)
    has_up = plane < planes - 1
    has_down = plane > 0

    direct = DEPTH_CHUNKS - SIDE_CHUNKS
    patches_copy = pltpu.make_async_copy(patches_ref, hidden, l_sem.at[4])

    @pl.when(pipe == 0)
    def _():
        patches_copy.start()

    small_copies = [
        pltpu.make_async_copy(there, here, l_sem.at[5 + index])
        for index, (there, here) in enumerate(
            (
                (gain_hbm, gain_ref),
                (shift_hbm, shift_ref),
                (out_shift_hbm, out_shift_ref),
                (layer_scale_hbm, layer_scale_ref),
            )
        )
    ]
    for small_copy in small_copies:
        small_copy.start()
    out_w_copy = pltpu.make_async_copy(out_w_ref, out_w, l_sem.at[0])
    out_w_copy.start()

    def owner_of(part):
        return (part * 4 + ctx) // group_blocks

    def own_column(part):
        return pl.multiple_of(((part * 4 + ctx) % group_blocks) * group, group)

    for part in range(PARTS):
        own_copy = pltpu.make_async_copy(
            w_ref.at[:, pl.ds(own_column(part), group)], weights.at[part], l_sem.at[1 + part]
        )

        @pl.when(owner_of(part) == plane)
        def _(own_copy=own_copy):
            own_copy.start()

    barrier = pltpu.get_barrier_semaphore()
    pl.semaphore_signal(barrier, inc=1, device_id={"pipe": 1 - pipe}, device_id_type=MESH)
    for other in others:
        pl.semaphore_signal(barrier, inc=1, device_id={"ctx": other}, device_id_type=MESH)

    @pl.when(has_up)
    def _():
        pl.semaphore_signal(barrier, inc=1, device_id={"dp": plane + 1}, device_id_type=MESH)

    @pl.when(has_down)
    def _():
        pl.semaphore_signal(barrier, inc=1, device_id={"dp": plane - 1}, device_id_type=MESH)

    def normalize_piece(at):
        span = pl.ds(at * piece, piece)
        normed[ctx, span, :] = normalize(hidden[span, :], gain_ref[...], shift_ref[...])

    for small_copy in small_copies:
        small_copy.wait()

    @pl.when(pipe == 0)
    def _():
        patches_copy.wait()
        for at in range(ROW_CHUNKS):
            normalize_piece(at)

    pl.semaphore_wait(barrier, 4 + has_up.astype(jnp.int32) + has_down.astype(jnp.int32))

    def w_copy(part, at, own, up):
        span = pl.ds(at * depth, depth)
        there = weights.at[part, span, :]
        here = w_ref.at[span, pl.ds(own_column(part), group)] if own else there
        return pltpu.make_async_remote_copy(
            src_ref=here,
            dst_ref=there,
            send_sem=(w_up if up else w_down).at[part, at],
            recv_sem=w_recv.at[part, at],
            device_id={"dp": plane + 1 if up else plane - 1},
            device_id_type=MESH,
        )

    def start_own(part, at):
        is_own = owner_of(part) == plane

        @pl.when(is_own & has_up)
        def _():
            w_copy(part, at, True, True).start()

        @pl.when(is_own & has_down)
        def _():
            w_copy(part, at, True, False).start()

    def relay(part, at):
        owner = owner_of(part)

        @pl.when(owner != plane)
        def _():
            w_copy(part, at, False, True).wait_recv()

        @pl.when((owner < plane) & has_up)
        def _():
            w_copy(part, at, False, True).start()

        @pl.when((owner > plane) & has_down)
        def _():
            w_copy(part, at, False, False).start()

    def cross_in(part, side):
        span = pl.ds((direct + side) * depth, depth)
        return pltpu.make_async_remote_copy(
            src_ref=w_ref.at[span, pl.ds(own_column(part), group)],
            dst_ref=side_weights.at[part, pl.ds(side * depth, depth), :],
            send_sem=b_cross.at[part, side],
            recv_sem=b_recv.at[part, side],
            device_id={"pipe": 1 - pipe},
            device_id_type=MESH,
        )

    def side_copy(part, side, up):
        block = side_weights.at[part, pl.ds(side * depth, depth), :]
        return pltpu.make_async_remote_copy(
            src_ref=block,
            dst_ref=block,
            send_sem=(b_up if up else b_down).at[part, side],
            recv_sem=b_recv.at[part, side],
            device_id={"dp": plane + 1 if up else plane - 1},
            device_id_type=MESH,
        )

    def cross_out(part, side):
        at = direct + side
        return pltpu.make_async_remote_copy(
            src_ref=side_weights.at[part, pl.ds(side * depth, depth), :],
            dst_ref=weights.at[part, pl.ds(at * depth, depth), :],
            send_sem=b_cross.at[part, side],
            recv_sem=w_recv.at[part, at],
            device_id={"pipe": 1 - pipe},
            device_id_type=MESH,
        )

    def relay_side(part, side):
        owner = owner_of(part)
        side_copy(part, side, True).wait_recv()

        @pl.when((owner <= plane) & has_up)
        def _():
            side_copy(part, side, True).start()

        @pl.when((owner >= plane) & has_down)
        def _():
            side_copy(part, side, False).start()

        @pl.when(owner != plane)
        def _():
            cross_out(part, side).start()

    @pl.when(pipe == 0)
    def _():
        for at in range(direct):
            for part in range(PARTS):
                if at < SIDE_CHUNKS:

                    @pl.when(owner_of(part) == plane)
                    def _(part=part, at=at):
                        cross_in(part, at).start()

                start_own(part, at)

    def t_copy(which, at):
        whose = across if which == 2 else ctx
        block = normed.at[whose, pl.ds(at * piece, piece), :]
        return pltpu.make_async_remote_copy(
            src_ref=block,
            dst_ref=block,
            send_sem=t_send.at[which, at],
            recv_sem=t_recv.at[which, at],
            device_id={"ctx": across if which == 1 else near},
            device_id_type=MESH,
        )

    def send_piece(at):
        t_copy(1, at).start()
        t_copy(0, at).start()

    def pass_pieces():
        for at in range(ROW_CHUNKS):
            t_copy(1, at).wait_recv()
            t_copy(2, at).start()

    @pl.when(pipe == 0)
    def _():
        for at in range(ROW_CHUNKS):
            send_piece(at)
        for at in range(direct):
            for part in range(PARTS):
                relay(part, at)
            if at == direct // 2:
                pass_pieces()
        for side in range(SIDE_CHUNKS):
            for part in range(PARTS):

                @pl.when(owner_of(part) != plane)
                def _(part=part, side=side):
                    cross_out(part, side).wait_recv()

    @pl.when(pipe == 1)
    def _():
        for side in range(SIDE_CHUNKS):
            for part in range(PARTS):
                relay_side(part, side)
        for at in range(DEPTH_CHUNKS):
            for part in range(PARTS):
                start_own(part, at)
        for at in range(DEPTH_CHUNKS):
            for part in range(PARTS):
                relay(part, at)

    def p_copy(at):
        block = hidden.at[pl.ds(at * piece, piece), :]
        return pltpu.make_async_remote_copy(
            src_ref=block,
            dst_ref=block,
            send_sem=p_send.at[at],
            recv_sem=p_recv.at[at],
            device_id={"pipe": 1 - pipe},
            device_id_type=MESH,
        )

    for part in range(PARTS):
        own_copy = pltpu.make_async_copy(
            w_ref.at[:, pl.ds(own_column(part), group)], weights.at[part], l_sem.at[1 + part]
        )

        @pl.when(owner_of(part) == plane)
        def _(own_copy=own_copy):
            own_copy.wait()

    @pl.when(pipe == 1)
    def _():
        for at in range(ROW_CHUNKS):
            p_copy(at).wait_recv()
            normalize_piece(at)
            send_piece(at)
        pass_pieces()

    for at in range(ROW_CHUNKS):
        t_copy(0, at).wait_recv()
        t_copy(2, at).wait_recv()

    total = 4 * rows
    tokens = normed[...].reshape(total, width)

    def project(part):
        return jnp.dot(tokens, weights[part], preferred_element_type=jnp.float32)

    queries = (project(0).astype(jnp.bfloat16) * jnp.bfloat16(head_width**-0.5)).astype(
        jnp.bfloat16
    )
    key_rows = project(1).astype(jnp.bfloat16)
    value_columns = project(2).T.astype(jnp.bfloat16)
    key_bias = jnp.where(
        lax.broadcasted_iota(jnp.int32, (total, 1), 0) < length_ref[0, 0], 0.0, masked_score
    )
    lane_head = lax.broadcasted_iota(jnp.int32, (total, 128), 1) // head_width

    def c_copy(other, which, pair):
        lanes = pl.ds(pair * 128, 128)
        return pltpu.make_async_remote_copy(
            src_ref=mine.at[pl.ds(pl.multiple_of(other * rows, rows), rows), lanes],
            dst_ref=gathered.at[ctx, :, lanes],
            send_sem=c_send.at[which, pair],
            recv_sem=c_recv.at[which, pair],
            device_id={"ctx": other},
            device_id_type=MESH,
        )

    per_pair = 128 // head_width
    for pair in range(pairs):
        pair_queries = queries[:, pair * 128 : (pair + 1) * 128]
        pair_keys = key_rows[:, pair * 128 : (pair + 1) * 128]
        columns = []
        for head in range(per_pair):
            head_queries = jnp.where(lane_head == head, pair_queries, jnp.bfloat16(0))
            scores = lax.dot_general(
                pair_keys,
                head_queries,
                (((1,), (1,)), ((), ())),
                preferred_element_type=jnp.float32,
            )
            scores = scores + key_bias
            top = jnp.max(scores, axis=0, keepdims=True)
            exps = jnp.exp(scores - top)
            totals = jnp.sum(exps, axis=0, keepdims=True)
            first = (pair * per_pair + head) * head_width
            part_sum = jnp.dot(
                value_columns[first : first + head_width, :],
                exps.astype(jnp.bfloat16),
                preferred_element_type=jnp.float32,
            )
            columns.append(part_sum / totals)
        context = jnp.concatenate(columns, axis=0).T.astype(jnp.bfloat16)
        mine[:, pair * 128 : (pair + 1) * 128] = context
        for which, other in ((1, across), (2, diagonal), (0, near)):
            c_copy(other, which, pair).start()

    own_rows = pl.ds(pl.multiple_of(ctx * rows, rows), rows)
    out_w_copy.wait()

    def out_part(block, whose):
        span = pl.ds(pl.multiple_of(whose * group, group), group)
        return jnp.dot(block, out_w[span, :], preferred_element_type=jnp.float32)

    mixed = out_part(mine[own_rows, :], ctx)
    for which, other in enumerate(others):
        for pair in range(pairs):
            c_copy(other, which, pair).wait_recv()
        mixed = mixed + out_part(gathered[other], other)
    mixed = mixed + out_shift_ref[...]
    produced = (
        hidden[...].astype(jnp.float32) + layer_scale_ref[...] * mixed
    ).astype(jnp.bfloat16)
    result_ref[...] = produced

    @pl.when(pipe == 0)
    def _():
        hidden[...] = produced
        for at in range(ROW_CHUNKS):
            p_copy(at).start()

    def sent(part, at):
        owner = owner_of(part)

        @pl.when((owner <= plane) & has_up)
        def _():
            w_copy(part, at, False, True).wait_send()

        @pl.when((owner >= plane) & has_down)
        def _():
            w_copy(part, at, False, False).wait_send()

    def sent_side(part, side):
        owner = owner_of(part)

        @pl.when((owner <= plane) & has_up)
        def _():
            side_copy(part, side, True).wait_send()

        @pl.when((owner >= plane) & has_down)
        def _():
            side_copy(part, side, False).wait_send()

        @pl.when(owner != plane)
        def _():
            cross_out(part, side).wait_send()

    for at in range(direct):
        for part in range(PARTS):
            sent(part, at)

    @pl.when(pipe == 0)
    def _():
        for side in range(SIDE_CHUNKS):
            for part in range(PARTS):

                @pl.when(owner_of(part) == plane)
                def _(part=part, side=side):
                    cross_in(part, side).wait_send()

    @pl.when(pipe == 1)
    def _():
        for at in range(direct, DEPTH_CHUNKS):
            for part in range(PARTS):
                sent(part, at)
        for side in range(SIDE_CHUNKS):
            for part in range(PARTS):
                sent_side(part, side)

    for at in range(ROW_CHUNKS):
        for which in range(3):
            t_copy(which, at).wait_send()
    for pair in range(pairs):
        for which, other in enumerate(others):
            c_copy(other, which, pair).wait_send()

    @pl.when(pipe == 0)
    def _():
        for at in range(ROW_CHUNKS):
            p_copy(at).wait_send()


def fused_device(
    mesh, patches, lengths, norm_gain, norm_bias, w_qkv, w_out, out_bias, scale_gain
):
    planes, groups = mesh.shape["dp"], mesh.shape["ctx"]
    micro_count, _, rows, width = patches.shape
    group = width // groups
    fits = (
        micro_count == 1
        and mesh.shape["pipe"] == 2
        and groups == 4
        and group % 128 == 0
        and 128 % (width // HEADS) == 0
        and w_qkv.shape[2] % group == 0
        and rows % (16 * ROW_CHUNKS) == 0
        and rows <= 128
    )
    if not fits:
        return per_device(
            patches, lengths, norm_gain, norm_bias, w_qkv, w_out, out_bias, scale_gain
        )
    bf16 = jnp.bfloat16
    pairs = group // 128
    vmem = pl.BlockSpec(memory_space=pltpu.VMEM)
    hbm = pl.BlockSpec(memory_space=pl.ANY)
    dma = pltpu.SemaphoreType.DMA
    result = pl.pallas_call(
        functools.partial(fused_kernel, (rows, width, planes, group)),
        out_shape=jax.ShapeDtypeStruct((rows, width), bf16),
        in_specs=[
            pl.BlockSpec(memory_space=pltpu.SMEM),
            hbm,
            hbm,
            hbm,
            hbm,
            hbm,
            hbm,
            hbm,
        ],
        out_specs=vmem,
        scratch_shapes=[
            pltpu.VMEM((1, width), jnp.float32),
            pltpu.VMEM((1, width), jnp.float32),
            pltpu.VMEM((1, width), jnp.float32),
            pltpu.VMEM((1, width), jnp.float32),
            pltpu.VMEM((PARTS, width // DEPTH_CHUNKS * SIDE_CHUNKS, group), bf16),
            pltpu.VMEM((rows, width), bf16),
            pltpu.VMEM((groups, rows, width), bf16),
            pltpu.VMEM((PARTS, width, group), bf16),
            pltpu.VMEM((width, width), bf16),
            pltpu.VMEM((groups * rows, group), bf16),
            pltpu.VMEM((groups, rows, group), bf16),
            dma((PARTS, DEPTH_CHUNKS)),
            dma((PARTS, DEPTH_CHUNKS)),
            dma((PARTS, DEPTH_CHUNKS)),
            dma((3, ROW_CHUNKS)),
            dma((3, ROW_CHUNKS)),
            dma((3, pairs)),
            dma((3, pairs)),
            dma((ROW_CHUNKS,)),
            dma((ROW_CHUNKS,)),
            dma((PARTS, SIDE_CHUNKS)),
            dma((PARTS, SIDE_CHUNKS)),
            dma((PARTS, SIDE_CHUNKS)),
            dma((PARTS, SIDE_CHUNKS)),
            dma((9,)),
        ],
        compiler_params=pltpu.CompilerParams(
            collective_id=0, has_side_effects=True, vmem_limit_bytes=62 * 1024 * 1024
        ),
    )(
        lengths,
        patches[0, 0],
        norm_gain,
        norm_bias,
        w_qkv[0],
        w_out[0],
        out_bias,
        scale_gain,
    )
    return result[None, None, None]


def solution(mesh):
    in_specs = (
        P(None, "dp", "ctx", None),
        P(None, "dp"),
        P("pipe", None),
        P("pipe", None),
        P("pipe", None, "dp"),
        P("pipe", None, None),
        P("pipe", None),
        P("pipe", None),
    )
    out_specs = P("pipe", None, "dp", "ctx", None)
    body = functools.partial(fused_device, mesh)
    return jax.shard_map(
        body, mesh=mesh, in_specs=in_specs, out_specs=out_specs, check_vma=False
    )
```

```python
import functools
import math

import jax
import jax.numpy as jnp
from jax import lax
from jax.experimental import pallas as pl
from jax.experimental.pallas import tpu as pltpu
from jax.sharding import PartitionSpec as P

HEADS = 16


epsilon = 1e-06
masked_score = -1e30


def shifted(value, axis, by):
    count = lax.axis_size(axis)
    pairs = [(i, i + by) for i in range(count) if 0 <= i + by < count]
    return lax.ppermute(value, axis, pairs)


def normalize(hidden, gain, shift):
    values = hidden.astype(jnp.float32)
    row_mean = jnp.mean(values, axis=-1, keepdims=True)
    centered = values - row_mean
    variance = jnp.mean(centered * centered, axis=-1, keepdims=True)
    return (centered * lax.rsqrt(variance + epsilon) * gain + shift).astype(jnp.bfloat16)


def per_device(patches, lengths, norm_gain, norm_bias, w_qkv, w_out, out_bias, scale_gain):
    section_index = lax.axis_index("pipe")
    section_count = lax.axis_size("pipe")
    group_count = lax.axis_size("ctx")
    micro_count = patches.shape[0]
    tok_rows = patches.shape[2]
    width = patches.shape[3]
    head_count = HEADS
    head_width = width // head_count
    group_heads = head_count // group_count
    score_scale = head_width ** (-0.5)
    qkv_full = lax.all_gather(w_qkv[0], "dp", axis=1, tiled=True)
    out_full = w_out[0]
    gain = norm_gain[0]
    shift = norm_bias[0]
    out_shift = out_bias[0]
    layer_scale = scale_gain[0]
    turn_count = micro_count + section_count - 1
    received = jnp.zeros((tok_rows, width), jnp.bfloat16)
    results = jnp.zeros((micro_count, tok_rows, width), jnp.bfloat16)
    volume_lengths = lengths[:, 0]
    for turn_index in range(turn_count):
        fresh = patches[min(turn_index, micro_count - 1), 0]
        current = jnp.where(section_index == 0, fresh, received)
        offset_turn = turn_index - section_index
        slot_index = jnp.clip(offset_turn, 0, micro_count - 1)
        length = lax.dynamic_index_in_dim(volume_lengths, slot_index, keepdims=False)
        normed = normalize(current, gain, shift)
        run_projected = jnp.dot(normed, qkv_full, preferred_element_type=jnp.float32).astype(
            jnp.bfloat16
        )
        run_projected = run_projected.reshape(tok_rows, 3, head_count, head_width)
        split_heads = run_projected.reshape(tok_rows, 3, group_count, group_heads, head_width)
        block = lax.all_to_all(split_heads, "ctx", split_axis=2, concat_axis=0, tiled=True)
        queries = block[:, 0, 0]
        key_rows = block[:, 1, 0]
        value_rows = block[:, 2, 0]
        total_rows = key_rows.shape[0]
        local_heads = queries.shape[1]
        valid = jnp.arange(total_rows, dtype=jnp.int32) < length
        query_block = math.gcd(total_rows, 512)
        grouped = queries.reshape(total_rows // query_block, query_block, local_heads, head_width)

        def one_block(query_group):
            scores = (
                jnp.einsum(
                    "qhd,khd->hqk", query_group, key_rows, preferred_element_type=jnp.float32
                )
                * score_scale
            )
            scores = jnp.where(valid[None, None, :], scores, masked_score)
            top_score = jnp.max(scores, axis=-1, keepdims=True)
            weights = jnp.where(valid[None, None, :], jnp.exp(scores - top_score), 0.0)
            totals = jnp.sum(weights, axis=-1)
            context = (
                jnp.einsum(
                    "hqk,khd->qhd",
                    weights.astype(jnp.bfloat16),
                    value_rows,
                    preferred_element_type=jnp.float32,
                )
                / totals.T[:, :, None]
            )
            return context.astype(jnp.bfloat16)

        blocks_out = lax.map(one_block, grouped)
        per_head = blocks_out.reshape(total_rows, 1, local_heads, head_width)
        merged = lax.all_to_all(per_head, "ctx", split_axis=0, concat_axis=1, tiled=True)
        run_context = merged.reshape(tok_rows, head_count, head_width)
        run_context = run_context.reshape(tok_rows, width)
        mixed = jnp.dot(run_context, out_full, preferred_element_type=jnp.float32) + out_shift
        produced = (current.astype(jnp.float32) + layer_scale * mixed).astype(jnp.bfloat16)
        keep_it = (offset_turn >= 0) & (offset_turn < micro_count)
        previous = lax.dynamic_index_in_dim(results, slot_index, keepdims=False)
        results = lax.dynamic_update_index_in_dim(
            results, jnp.where(keep_it, produced, previous), slot_index, 0
        )
        if turn_index + 1 < turn_count:
            received = shifted(produced, "pipe", 1)
    return results[None, :, None]


MESH = pl.DeviceIdType.MESH
PARTS = 3
DEPTH_CHUNKS = 4
SIDE_CHUNKS = 1
ROW_CHUNKS = 2


def fused_kernel(
    sizes,
    length_ref,
    patches_ref,
    gain_hbm,
    shift_hbm,
    w_ref,
    out_w_ref,
    out_shift_hbm,
    layer_scale_hbm,
    result_ref,
    gain_ref,
    shift_ref,
    out_shift_ref,
    layer_scale_ref,
    side_weights,
    hidden,
    normed,
    weights,
    out_w,
    mine,
    gathered,
    w_recv,
    w_up,
    w_down,
    t_send,
    t_recv,
    c_send,
    c_recv,
    p_send,
    p_recv,
    b_recv,
    b_up,
    b_down,
    b_cross,
    l_sem,
):
    rows, width, planes, group = sizes
    head_width = width // HEADS
    group_blocks = w_ref.shape[1] // group
    depth = width // DEPTH_CHUNKS
    piece = rows // ROW_CHUNKS
    pairs = group // 128
    pipe = lax.axis_index("pipe")
    ctx = lax.axis_index("ctx")
    plane = lax.axis_index("dp")
    core, side = ctx % 2, ctx // 2
    near = side * 2 + (1 - core)
    across = (1 - side) * 2 + core
    diagonal = 3 - ctx
    others = (near, across, diagonal)
    has_up = plane < planes - 1
    has_down = plane > 0

    direct = DEPTH_CHUNKS - SIDE_CHUNKS
    patches_copy = pltpu.make_async_copy(patches_ref, hidden, l_sem.at[4])

    @pl.when(pipe == 0)
    def _():
        patches_copy.start()

    small_copies = [
        pltpu.make_async_copy(there, here, l_sem.at[5 + index])
        for index, (there, here) in enumerate(
            (
                (gain_hbm, gain_ref),
                (shift_hbm, shift_ref),
                (out_shift_hbm, out_shift_ref),
                (layer_scale_hbm, layer_scale_ref),
            )
        )
    ]
    for small_copy in small_copies:
        small_copy.start()
    out_w_copy = pltpu.make_async_copy(out_w_ref, out_w, l_sem.at[0])
    out_w_copy.start()

    def owner_of(part):
        return (part * 4 + ctx) // group_blocks

    def own_column(part):
        return pl.multiple_of(((part * 4 + ctx) % group_blocks) * group, group)

    for part in range(PARTS):
        own_copy = pltpu.make_async_copy(
            w_ref.at[:, pl.ds(own_column(part), group)], weights.at[part], l_sem.at[1 + part]
        )

        @pl.when(owner_of(part) == plane)
        def _(own_copy=own_copy):
            own_copy.start()

    barrier = pltpu.get_barrier_semaphore()
    pl.semaphore_signal(barrier, inc=1, device_id={"pipe": 1 - pipe}, device_id_type=MESH)
    for other in others:
        pl.semaphore_signal(barrier, inc=1, device_id={"ctx": other}, device_id_type=MESH)

    @pl.when(has_up)
    def _():
        pl.semaphore_signal(barrier, inc=1, device_id={"dp": plane + 1}, device_id_type=MESH)

    @pl.when(has_down)
    def _():
        pl.semaphore_signal(barrier, inc=1, device_id={"dp": plane - 1}, device_id_type=MESH)

    def normalize_piece(at):
        span = pl.ds(at * piece, piece)
        normed[ctx, span, :] = normalize(hidden[span, :], gain_ref[...], shift_ref[...])

    for small_copy in small_copies:
        small_copy.wait()

    @pl.when(pipe == 0)
    def _():
        patches_copy.wait()
        for at in range(ROW_CHUNKS):
            normalize_piece(at)

    for part in range(PARTS):
        own_copy = pltpu.make_async_copy(
            w_ref.at[:, pl.ds(own_column(part), group)], weights.at[part], l_sem.at[1 + part]
        )

        @pl.when(owner_of(part) == plane)
        def _(own_copy=own_copy):
            own_copy.wait()

    pl.semaphore_wait(barrier, 4 + has_up.astype(jnp.int32) + has_down.astype(jnp.int32))

    def w_copy(part, at, up):
        span = pl.ds(at * depth, depth)
        there = weights.at[part, span, :]
        return pltpu.make_async_remote_copy(
            src_ref=there,
            dst_ref=there,
            send_sem=(w_up if up else w_down).at[part, at],
            recv_sem=w_recv.at[part, at],
            device_id={"dp": plane + 1 if up else plane - 1},
            device_id_type=MESH,
        )

    def start_own(part, at):
        is_own = owner_of(part) == plane

        @pl.when(is_own & has_up)
        def _():
            w_copy(part, at, True).start()

        @pl.when(is_own & has_down)
        def _():
            w_copy(part, at, False).start()

    def relay(part, at):
        owner = owner_of(part)

        @pl.when(owner != plane)
        def _():
            w_copy(part, at, True).wait_recv()

        @pl.when((owner < plane) & has_up)
        def _():
            w_copy(part, at, True).start()

        @pl.when((owner > plane) & has_down)
        def _():
            w_copy(part, at, False).start()

    def cross_in(part, side):
        span = pl.ds((direct + side) * depth, depth)
        return pltpu.make_async_remote_copy(
            src_ref=weights.at[part, span, :],
            dst_ref=side_weights.at[part, pl.ds(side * depth, depth), :],
            send_sem=b_cross.at[part, side],
            recv_sem=b_recv.at[part, side],
            device_id={"pipe": 1 - pipe},
            device_id_type=MESH,
        )

    def side_copy(part, side, up):
        block = side_weights.at[part, pl.ds(side * depth, depth), :]
        return pltpu.make_async_remote_copy(
            src_ref=block,
            dst_ref=block,
            send_sem=(b_up if up else b_down).at[part, side],
            recv_sem=b_recv.at[part, side],
            device_id={"dp": plane + 1 if up else plane - 1},
            device_id_type=MESH,
        )

    def cross_out(part, side):
        at = direct + side
        return pltpu.make_async_remote_copy(
            src_ref=side_weights.at[part, pl.ds(side * depth, depth), :],
            dst_ref=weights.at[part, pl.ds(at * depth, depth), :],
            send_sem=b_cross.at[part, side],
            recv_sem=w_recv.at[part, at],
            device_id={"pipe": 1 - pipe},
            device_id_type=MESH,
        )

    def relay_side(part, side):
        owner = owner_of(part)
        side_copy(part, side, True).wait_recv()

        @pl.when((owner <= plane) & has_up)
        def _():
            side_copy(part, side, True).start()

        @pl.when((owner >= plane) & has_down)
        def _():
            side_copy(part, side, False).start()

        @pl.when(owner != plane)
        def _():
            cross_out(part, side).start()

    @pl.when(pipe == 0)
    def _():
        for at in range(direct):
            for part in range(PARTS):
                if at < SIDE_CHUNKS:

                    @pl.when(owner_of(part) == plane)
                    def _(part=part, at=at):
                        cross_in(part, at).start()

                start_own(part, at)

    def t_copy(which, at):
        whose = across if which == 2 else ctx
        block = normed.at[whose, pl.ds(at * piece, piece), :]
        return pltpu.make_async_remote_copy(
            src_ref=block,
            dst_ref=block,
            send_sem=t_send.at[which, at],
            recv_sem=t_recv.at[which, at],
            device_id={"ctx": across if which == 1 else near},
            device_id_type=MESH,
        )

    def send_piece(at):
        t_copy(1, at).start()
        t_copy(0, at).start()

    def pass_pieces():
        for at in range(ROW_CHUNKS):
            t_copy(1, at).wait_recv()
            t_copy(2, at).start()

    @pl.when(pipe == 0)
    def _():
        for at in range(ROW_CHUNKS):
            send_piece(at)
        for at in range(direct):
            for part in range(PARTS):
                relay(part, at)
            if at == direct // 2:
                pass_pieces()
        for side in range(SIDE_CHUNKS):
            for part in range(PARTS):

                @pl.when(owner_of(part) != plane)
                def _(part=part, side=side):
                    cross_out(part, side).wait_recv()

    @pl.when(pipe == 1)
    def _():
        for side in range(SIDE_CHUNKS):
            for part in range(PARTS):
                relay_side(part, side)
        for at in range(DEPTH_CHUNKS):
            for part in range(PARTS):
                start_own(part, at)
        for at in range(DEPTH_CHUNKS):
            for part in range(PARTS):
                relay(part, at)

    def p_copy(at):
        block = hidden.at[pl.ds(at * piece, piece), :]
        return pltpu.make_async_remote_copy(
            src_ref=block,
            dst_ref=block,
            send_sem=p_send.at[at],
            recv_sem=p_recv.at[at],
            device_id={"pipe": 1 - pipe},
            device_id_type=MESH,
        )

    @pl.when(pipe == 1)
    def _():
        for at in range(ROW_CHUNKS):
            p_copy(at).wait_recv()
            normalize_piece(at)
            send_piece(at)
        pass_pieces()

    for at in range(ROW_CHUNKS):
        t_copy(0, at).wait_recv()
        t_copy(2, at).wait_recv()

    total = 4 * rows
    tokens = normed[...].reshape(total, width)

    def project(part):
        return jnp.dot(tokens, weights[part], preferred_element_type=jnp.float32)

    queries = (project(0).astype(jnp.bfloat16) * jnp.bfloat16(head_width**-0.5)).astype(
        jnp.bfloat16
    )
    key_rows = project(1).astype(jnp.bfloat16)
    value_columns = project(2).T.astype(jnp.bfloat16)
    key_bias = jnp.where(
        lax.broadcasted_iota(jnp.int32, (total, 1), 0) < length_ref[0, 0], 0.0, masked_score
    )
    lane_head = lax.broadcasted_iota(jnp.int32, (total, 128), 1) // head_width

    def c_copy(other, which, pair):
        lanes = pl.ds(pair * 128, 128)
        return pltpu.make_async_remote_copy(
            src_ref=mine.at[pl.ds(pl.multiple_of(other * rows, rows), rows), lanes],
            dst_ref=gathered.at[ctx, :, lanes],
            send_sem=c_send.at[which, pair],
            recv_sem=c_recv.at[which, pair],
            device_id={"ctx": other},
            device_id_type=MESH,
        )

    per_pair = 128 // head_width
    for pair in range(pairs):
        pair_queries = queries[:, pair * 128 : (pair + 1) * 128]
        pair_keys = key_rows[:, pair * 128 : (pair + 1) * 128]
        columns = []
        for head in range(per_pair):
            head_queries = jnp.where(lane_head == head, pair_queries, jnp.bfloat16(0))
            scores = lax.dot_general(
                pair_keys,
                head_queries,
                (((1,), (1,)), ((), ())),
                preferred_element_type=jnp.float32,
            )
            scores = scores + key_bias
            top = jnp.max(scores, axis=0, keepdims=True)
            exps = jnp.exp(scores - top)
            totals = jnp.sum(exps, axis=0, keepdims=True)
            first = (pair * per_pair + head) * head_width
            part_sum = jnp.dot(
                value_columns[first : first + head_width, :],
                exps.astype(jnp.bfloat16),
                preferred_element_type=jnp.float32,
            )
            columns.append(part_sum / totals)
        context = jnp.concatenate(columns, axis=0).T.astype(jnp.bfloat16)
        mine[:, pair * 128 : (pair + 1) * 128] = context
        for which, other in ((1, across), (2, diagonal), (0, near)):
            c_copy(other, which, pair).start()

    own_rows = pl.ds(pl.multiple_of(ctx * rows, rows), rows)
    out_w_copy.wait()

    def out_part(block, whose):
        span = pl.ds(pl.multiple_of(whose * group, group), group)
        return jnp.dot(block, out_w[span, :], preferred_element_type=jnp.float32)

    mixed = out_part(mine[own_rows, :], ctx)
    for which, other in enumerate(others):
        for pair in range(pairs):
            c_copy(other, which, pair).wait_recv()
        mixed = mixed + out_part(gathered[other], other)
    mixed = mixed + out_shift_ref[...]
    produced = (
        hidden[...].astype(jnp.float32) + layer_scale_ref[...] * mixed
    ).astype(jnp.bfloat16)
    result_ref[...] = produced

    @pl.when(pipe == 0)
    def _():
        hidden[...] = produced
        for at in range(ROW_CHUNKS):
            p_copy(at).start()

    def sent(part, at):
        owner = owner_of(part)

        @pl.when((owner <= plane) & has_up)
        def _():
            w_copy(part, at, True).wait_send()

        @pl.when((owner >= plane) & has_down)
        def _():
            w_copy(part, at, False).wait_send()

    def sent_side(part, side):
        owner = owner_of(part)

        @pl.when((owner <= plane) & has_up)
        def _():
            side_copy(part, side, True).wait_send()

        @pl.when((owner >= plane) & has_down)
        def _():
            side_copy(part, side, False).wait_send()

        @pl.when(owner != plane)
        def _():
            cross_out(part, side).wait_send()

    for at in range(direct):
        for part in range(PARTS):
            sent(part, at)

    @pl.when(pipe == 0)
    def _():
        for side in range(SIDE_CHUNKS):
            for part in range(PARTS):

                @pl.when(owner_of(part) == plane)
                def _(part=part, side=side):
                    cross_in(part, side).wait_send()

    @pl.when(pipe == 1)
    def _():
        for at in range(direct, DEPTH_CHUNKS):
            for part in range(PARTS):
                sent(part, at)
        for side in range(SIDE_CHUNKS):
            for part in range(PARTS):
                sent_side(part, side)

    for at in range(ROW_CHUNKS):
        for which in range(3):
            t_copy(which, at).wait_send()
    for pair in range(pairs):
        for which, other in enumerate(others):
            c_copy(other, which, pair).wait_send()

    @pl.when(pipe == 0)
    def _():
        for at in range(ROW_CHUNKS):
            p_copy(at).wait_send()


def fused_device(
    mesh, patches, lengths, norm_gain, norm_bias, w_qkv, w_out, out_bias, scale_gain
):
    planes, groups = mesh.shape["dp"], mesh.shape["ctx"]
    micro_count, _, rows, width = patches.shape
    group = width // groups
    fits = (
        micro_count == 1
        and mesh.shape["pipe"] == 2
        and groups == 4
        and group % 128 == 0
        and 128 % (width // HEADS) == 0
        and w_qkv.shape[2] % group == 0
        and rows % (16 * ROW_CHUNKS) == 0
        and rows <= 128
    )
    if not fits:
        return per_device(
            patches, lengths, norm_gain, norm_bias, w_qkv, w_out, out_bias, scale_gain
        )
    bf16 = jnp.bfloat16
    pairs = group // 128
    vmem = pl.BlockSpec(memory_space=pltpu.VMEM)
    hbm = pl.BlockSpec(memory_space=pl.ANY)
    dma = pltpu.SemaphoreType.DMA
    result = pl.pallas_call(
        functools.partial(fused_kernel, (rows, width, planes, group)),
        out_shape=jax.ShapeDtypeStruct((rows, width), bf16),
        in_specs=[
            pl.BlockSpec(memory_space=pltpu.SMEM),
            hbm,
            hbm,
            hbm,
            hbm,
            hbm,
            hbm,
            hbm,
        ],
        out_specs=vmem,
        scratch_shapes=[
            pltpu.VMEM((1, width), jnp.float32),
            pltpu.VMEM((1, width), jnp.float32),
            pltpu.VMEM((1, width), jnp.float32),
            pltpu.VMEM((1, width), jnp.float32),
            pltpu.VMEM((PARTS, width // DEPTH_CHUNKS * SIDE_CHUNKS, group), bf16),
            pltpu.VMEM((rows, width), bf16),
            pltpu.VMEM((groups, rows, width), bf16),
            pltpu.VMEM((PARTS, width, group), bf16),
            pltpu.VMEM((width, width), bf16),
            pltpu.VMEM((groups * rows, group), bf16),
            pltpu.VMEM((groups, rows, group), bf16),
            dma((PARTS, DEPTH_CHUNKS)),
            dma((PARTS, DEPTH_CHUNKS)),
            dma((PARTS, DEPTH_CHUNKS)),
            dma((3, ROW_CHUNKS)),
            dma((3, ROW_CHUNKS)),
            dma((3, pairs)),
            dma((3, pairs)),
            dma((ROW_CHUNKS,)),
            dma((ROW_CHUNKS,)),
            dma((PARTS, SIDE_CHUNKS)),
            dma((PARTS, SIDE_CHUNKS)),
            dma((PARTS, SIDE_CHUNKS)),
            dma((PARTS, SIDE_CHUNKS)),
            dma((9,)),
        ],
        compiler_params=pltpu.CompilerParams(
            collective_id=0, has_side_effects=True, vmem_limit_bytes=62 * 1024 * 1024
        ),
    )(
        lengths,
        patches[0, 0],
        norm_gain,
        norm_bias,
        w_qkv[0],
        w_out[0],
        out_bias,
        scale_gain,
    )
    return result[None, None, None]


def solution(mesh):
    in_specs = (
        P(None, "dp", "ctx", None),
        P(None, "dp"),
        P("pipe", None),
        P("pipe", None),
        P("pipe", None, "dp"),
        P("pipe", None, None),
        P("pipe", None),
        P("pipe", None),
    )
    out_specs = P("pipe", None, "dp", "ctx", None)
    body = functools.partial(fused_device, mesh)
    return jax.shard_map(
        body, mesh=mesh, in_specs=in_specs, out_specs=out_specs, check_vma=False
    )
```

```python
import functools
import math

import jax
import jax.numpy as jnp
from jax import lax
from jax.experimental import pallas as pl
from jax.experimental.pallas import tpu as pltpu
from jax.sharding import PartitionSpec as P

HEADS = 16


epsilon = 1e-06
masked_score = -1e30


def shifted(value, axis, by):
    count = lax.axis_size(axis)
    pairs = [(i, i + by) for i in range(count) if 0 <= i + by < count]
    return lax.ppermute(value, axis, pairs)


def normalize(hidden, gain, shift):
    values = hidden.astype(jnp.float32)
    row_mean = jnp.mean(values, axis=-1, keepdims=True)
    centered = values - row_mean
    variance = jnp.mean(centered * centered, axis=-1, keepdims=True)
    return (centered * lax.rsqrt(variance + epsilon) * gain + shift).astype(jnp.bfloat16)


def per_device(patches, lengths, norm_gain, norm_bias, w_qkv, w_out, out_bias, scale_gain):
    section_index = lax.axis_index("pipe")
    section_count = lax.axis_size("pipe")
    group_count = lax.axis_size("ctx")
    micro_count = patches.shape[0]
    tok_rows = patches.shape[2]
    width = patches.shape[3]
    head_count = HEADS
    head_width = width // head_count
    group_heads = head_count // group_count
    score_scale = head_width ** (-0.5)
    qkv_full = lax.all_gather(w_qkv[0], "dp", axis=1, tiled=True)
    out_full = w_out[0]
    gain = norm_gain[0]
    shift = norm_bias[0]
    out_shift = out_bias[0]
    layer_scale = scale_gain[0]
    turn_count = micro_count + section_count - 1
    received = jnp.zeros((tok_rows, width), jnp.bfloat16)
    results = jnp.zeros((micro_count, tok_rows, width), jnp.bfloat16)
    volume_lengths = lengths[:, 0]
    for turn_index in range(turn_count):
        fresh = patches[min(turn_index, micro_count - 1), 0]
        current = jnp.where(section_index == 0, fresh, received)
        offset_turn = turn_index - section_index
        slot_index = jnp.clip(offset_turn, 0, micro_count - 1)
        length = lax.dynamic_index_in_dim(volume_lengths, slot_index, keepdims=False)
        normed = normalize(current, gain, shift)
        run_projected = jnp.dot(normed, qkv_full, preferred_element_type=jnp.float32).astype(
            jnp.bfloat16
        )
        run_projected = run_projected.reshape(tok_rows, 3, head_count, head_width)
        split_heads = run_projected.reshape(tok_rows, 3, group_count, group_heads, head_width)
        block = lax.all_to_all(split_heads, "ctx", split_axis=2, concat_axis=0, tiled=True)
        queries = block[:, 0, 0]
        key_rows = block[:, 1, 0]
        value_rows = block[:, 2, 0]
        total_rows = key_rows.shape[0]
        local_heads = queries.shape[1]
        valid = jnp.arange(total_rows, dtype=jnp.int32) < length
        query_block = math.gcd(total_rows, 512)
        grouped = queries.reshape(total_rows // query_block, query_block, local_heads, head_width)

        def one_block(query_group):
            scores = (
                jnp.einsum(
                    "qhd,khd->hqk", query_group, key_rows, preferred_element_type=jnp.float32
                )
                * score_scale
            )
            scores = jnp.where(valid[None, None, :], scores, masked_score)
            top_score = jnp.max(scores, axis=-1, keepdims=True)
            weights = jnp.where(valid[None, None, :], jnp.exp(scores - top_score), 0.0)
            totals = jnp.sum(weights, axis=-1)
            context = (
                jnp.einsum(
                    "hqk,khd->qhd",
                    weights.astype(jnp.bfloat16),
                    value_rows,
                    preferred_element_type=jnp.float32,
                )
                / totals.T[:, :, None]
            )
            return context.astype(jnp.bfloat16)

        blocks_out = lax.map(one_block, grouped)
        per_head = blocks_out.reshape(total_rows, 1, local_heads, head_width)
        merged = lax.all_to_all(per_head, "ctx", split_axis=0, concat_axis=1, tiled=True)
        run_context = merged.reshape(tok_rows, head_count, head_width)
        run_context = run_context.reshape(tok_rows, width)
        mixed = jnp.dot(run_context, out_full, preferred_element_type=jnp.float32) + out_shift
        produced = (current.astype(jnp.float32) + layer_scale * mixed).astype(jnp.bfloat16)
        keep_it = (offset_turn >= 0) & (offset_turn < micro_count)
        previous = lax.dynamic_index_in_dim(results, slot_index, keepdims=False)
        results = lax.dynamic_update_index_in_dim(
            results, jnp.where(keep_it, produced, previous), slot_index, 0
        )
        if turn_index + 1 < turn_count:
            received = shifted(produced, "pipe", 1)
    return results[None, :, None]


MESH = pl.DeviceIdType.MESH
PARTS = 3
DEPTH_CHUNKS = 4
SIDE_CHUNKS = 1
ROW_CHUNKS = 2


def fused_kernel(
    sizes,
    length_ref,
    patches_ref,
    gain_hbm,
    shift_hbm,
    w_ref,
    out_w_ref,
    out_shift_hbm,
    layer_scale_hbm,
    result_ref,
    gain_ref,
    shift_ref,
    out_shift_ref,
    layer_scale_ref,
    side_weights,
    hidden,
    normed,
    weights,
    out_w,
    mine,
    gathered,
    w_recv,
    w_up,
    w_down,
    t_send,
    t_recv,
    c_send,
    c_recv,
    p_send,
    p_recv,
    b_recv,
    b_up,
    b_down,
    b_cross,
    l_sem,
):
    rows, width, planes, group = sizes
    head_width = width // HEADS
    group_blocks = w_ref.shape[1] // group
    depth = width // DEPTH_CHUNKS
    piece = rows // ROW_CHUNKS
    pairs = group // 128
    pipe = lax.axis_index("pipe")
    ctx = lax.axis_index("ctx")
    plane = lax.axis_index("dp")
    core, side = ctx % 2, ctx // 2
    near = side * 2 + (1 - core)
    across = (1 - side) * 2 + core
    diagonal = 3 - ctx
    others = (near, across, diagonal)
    has_up = plane < planes - 1
    has_down = plane > 0

    direct = DEPTH_CHUNKS - SIDE_CHUNKS
    patches_copy = pltpu.make_async_copy(patches_ref, hidden, l_sem.at[4])

    @pl.when(pipe == 0)
    def _():
        patches_copy.start()

    small_copies = [
        pltpu.make_async_copy(there, here, l_sem.at[5 + index])
        for index, (there, here) in enumerate(
            (
                (gain_hbm, gain_ref),
                (shift_hbm, shift_ref),
                (out_shift_hbm, out_shift_ref),
                (layer_scale_hbm, layer_scale_ref),
            )
        )
    ]
    for small_copy in small_copies:
        small_copy.start()
    out_w_copy = pltpu.make_async_copy(out_w_ref, out_w, l_sem.at[0])
    out_w_copy.start()

    def owner_of(part):
        return (part * 4 + ctx) // group_blocks

    def own_column(part):
        return pl.multiple_of(((part * 4 + ctx) % group_blocks) * group, group)

    for part in range(PARTS):
        own_copy = pltpu.make_async_copy(
            w_ref.at[:, pl.ds(own_column(part), group)], weights.at[part], l_sem.at[1 + part]
        )

        @pl.when(owner_of(part) == plane)
        def _(own_copy=own_copy):
            own_copy.start()

    barrier = pltpu.get_barrier_semaphore()
    pl.semaphore_signal(barrier, inc=1, device_id={"pipe": 1 - pipe}, device_id_type=MESH)
    for other in others:
        pl.semaphore_signal(barrier, inc=1, device_id={"ctx": other}, device_id_type=MESH)

    @pl.when(has_up)
    def _():
        pl.semaphore_signal(barrier, inc=1, device_id={"dp": plane + 1}, device_id_type=MESH)

    @pl.when(has_down)
    def _():
        pl.semaphore_signal(barrier, inc=1, device_id={"dp": plane - 1}, device_id_type=MESH)

    def normalize_piece(at):
        span = pl.ds(at * piece, piece)
        normed[ctx, span, :] = normalize(hidden[span, :], gain_ref[...], shift_ref[...])

    for small_copy in small_copies:
        small_copy.wait()

    @pl.when(pipe == 0)
    def _():
        patches_copy.wait()
        for at in range(ROW_CHUNKS):
            normalize_piece(at)

    for part in range(PARTS):
        own_copy = pltpu.make_async_copy(
            w_ref.at[:, pl.ds(own_column(part), group)], weights.at[part], l_sem.at[1 + part]
        )

        @pl.when(owner_of(part) == plane)
        def _(own_copy=own_copy):
            own_copy.wait()

    pl.semaphore_wait(barrier, 4 + has_up.astype(jnp.int32) + has_down.astype(jnp.int32))

    def w_copy(part, at, up):
        span = pl.ds(at * depth, depth)
        there = weights.at[part, span, :]
        return pltpu.make_async_remote_copy(
            src_ref=there,
            dst_ref=there,
            send_sem=(w_up if up else w_down).at[part, at],
            recv_sem=w_recv.at[part, at],
            device_id={"dp": plane + 1 if up else plane - 1},
            device_id_type=MESH,
        )

    def start_own(part, at):
        is_own = owner_of(part) == plane

        @pl.when(is_own & has_up)
        def _():
            w_copy(part, at, True).start()

        @pl.when(is_own & has_down)
        def _():
            w_copy(part, at, False).start()

    def relay(part, at):
        owner = owner_of(part)

        @pl.when(owner != plane)
        def _():
            w_copy(part, at, True).wait_recv()

        @pl.when((owner < plane) & has_up)
        def _():
            w_copy(part, at, True).start()

        @pl.when((owner > plane) & has_down)
        def _():
            w_copy(part, at, False).start()

    def distance(part):
        return jnp.abs(owner_of(part) - plane)

    def relay_from(away, count):
        for at in range(count):
            for part in range(PARTS):

                @pl.when(distance(part) == away)
                def _(part=part, at=at):
                    relay(part, at)

    def cross_in(part, side):
        span = pl.ds((direct + side) * depth, depth)
        return pltpu.make_async_remote_copy(
            src_ref=weights.at[part, span, :],
            dst_ref=side_weights.at[part, pl.ds(side * depth, depth), :],
            send_sem=b_cross.at[part, side],
            recv_sem=b_recv.at[part, side],
            device_id={"pipe": 1 - pipe},
            device_id_type=MESH,
        )

    def side_copy(part, side, up):
        block = side_weights.at[part, pl.ds(side * depth, depth), :]
        return pltpu.make_async_remote_copy(
            src_ref=block,
            dst_ref=block,
            send_sem=(b_up if up else b_down).at[part, side],
            recv_sem=b_recv.at[part, side],
            device_id={"dp": plane + 1 if up else plane - 1},
            device_id_type=MESH,
        )

    def cross_out(part, side):
        at = direct + side
        return pltpu.make_async_remote_copy(
            src_ref=side_weights.at[part, pl.ds(side * depth, depth), :],
            dst_ref=weights.at[part, pl.ds(at * depth, depth), :],
            send_sem=b_cross.at[part, side],
            recv_sem=w_recv.at[part, at],
            device_id={"pipe": 1 - pipe},
            device_id_type=MESH,
        )

    def relay_side(part, side):
        owner = owner_of(part)
        side_copy(part, side, True).wait_recv()

        @pl.when((owner <= plane) & has_up)
        def _():
            side_copy(part, side, True).start()

        @pl.when((owner >= plane) & has_down)
        def _():
            side_copy(part, side, False).start()

        @pl.when(owner != plane)
        def _():
            cross_out(part, side).start()

    @pl.when(pipe == 0)
    def _():
        for at in range(direct):
            for part in range(PARTS):
                if at < SIDE_CHUNKS:

                    @pl.when(owner_of(part) == plane)
                    def _(part=part, at=at):
                        cross_in(part, at).start()

                start_own(part, at)

    def t_copy(which, at):
        whose = across if which == 2 else ctx
        block = normed.at[whose, pl.ds(at * piece, piece), :]
        return pltpu.make_async_remote_copy(
            src_ref=block,
            dst_ref=block,
            send_sem=t_send.at[which, at],
            recv_sem=t_recv.at[which, at],
            device_id={"ctx": across if which == 1 else near},
            device_id_type=MESH,
        )

    def send_piece(at):
        t_copy(1, at).start()
        t_copy(0, at).start()

    def pass_pieces():
        for at in range(ROW_CHUNKS):
            t_copy(1, at).wait_recv()
            t_copy(2, at).start()

    @pl.when(pipe == 0)
    def _():
        for at in range(ROW_CHUNKS):
            send_piece(at)
        for away in range(1, planes):
            relay_from(away, direct)
            if away == 1:
                pass_pieces()
        for side in range(SIDE_CHUNKS):
            for part in range(PARTS):

                @pl.when(owner_of(part) != plane)
                def _(part=part, side=side):
                    cross_out(part, side).wait_recv()

    @pl.when(pipe == 1)
    def _():
        for away in range(planes):
            for side in range(SIDE_CHUNKS):
                for part in range(PARTS):

                    @pl.when(distance(part) == away)
                    def _(part=part, side=side):
                        relay_side(part, side)

            if away < 2:
                for part in range(PARTS):
                    start_own(part, away)
        for at in range(2, DEPTH_CHUNKS):
            for part in range(PARTS):
                start_own(part, at)
        for away in range(1, planes):
            relay_from(away, DEPTH_CHUNKS)

    def p_copy(at):
        block = hidden.at[pl.ds(at * piece, piece), :]
        return pltpu.make_async_remote_copy(
            src_ref=block,
            dst_ref=block,
            send_sem=p_send.at[at],
            recv_sem=p_recv.at[at],
            device_id={"pipe": 1 - pipe},
            device_id_type=MESH,
        )

    @pl.when(pipe == 1)
    def _():
        for at in range(ROW_CHUNKS):
            p_copy(at).wait_recv()
            normalize_piece(at)
            send_piece(at)
        pass_pieces()

    for at in range(ROW_CHUNKS):
        t_copy(0, at).wait_recv()
        t_copy(2, at).wait_recv()

    total = 4 * rows
    tokens = normed[...].reshape(total, width)

    def project(part):
        return jnp.dot(tokens, weights[part], preferred_element_type=jnp.float32)

    queries = (project(0).astype(jnp.bfloat16) * jnp.bfloat16(head_width**-0.5)).astype(
        jnp.bfloat16
    )
    key_rows = project(1).astype(jnp.bfloat16)
    value_columns = project(2).T.astype(jnp.bfloat16)
    key_bias = jnp.where(
        lax.broadcasted_iota(jnp.int32, (total, 1), 0) < length_ref[0, 0], 0.0, masked_score
    )
    lane_head = lax.broadcasted_iota(jnp.int32, (total, 128), 1) // head_width

    def c_copy(other, which, pair):
        lanes = pl.ds(pair * 128, 128)
        return pltpu.make_async_remote_copy(
            src_ref=mine.at[pl.ds(pl.multiple_of(other * rows, rows), rows), lanes],
            dst_ref=gathered.at[ctx, :, lanes],
            send_sem=c_send.at[which, pair],
            recv_sem=c_recv.at[which, pair],
            device_id={"ctx": other},
            device_id_type=MESH,
        )

    per_pair = 128 // head_width
    for pair in range(pairs):
        pair_queries = queries[:, pair * 128 : (pair + 1) * 128]
        pair_keys = key_rows[:, pair * 128 : (pair + 1) * 128]
        columns = []
        for head in range(per_pair):
            head_queries = jnp.where(lane_head == head, pair_queries, jnp.bfloat16(0))
            scores = lax.dot_general(
                pair_keys,
                head_queries,
                (((1,), (1,)), ((), ())),
                preferred_element_type=jnp.float32,
            )
            scores = scores + key_bias
            top = jnp.max(scores, axis=0, keepdims=True)
            exps = jnp.exp(scores - top)
            totals = jnp.sum(exps, axis=0, keepdims=True)
            first = (pair * per_pair + head) * head_width
            part_sum = jnp.dot(
                value_columns[first : first + head_width, :],
                exps.astype(jnp.bfloat16),
                preferred_element_type=jnp.float32,
            )
            columns.append(part_sum / totals)
        context = jnp.concatenate(columns, axis=0).T.astype(jnp.bfloat16)
        mine[:, pair * 128 : (pair + 1) * 128] = context
        for which, other in ((1, across), (2, diagonal), (0, near)):
            c_copy(other, which, pair).start()

    own_rows = pl.ds(pl.multiple_of(ctx * rows, rows), rows)
    out_w_copy.wait()

    def out_part(block, whose):
        span = pl.ds(pl.multiple_of(whose * group, group), group)
        return jnp.dot(block, out_w[span, :], preferred_element_type=jnp.float32)

    mixed = out_part(mine[own_rows, :], ctx)
    for which, other in enumerate(others):
        for pair in range(pairs):
            c_copy(other, which, pair).wait_recv()
        mixed = mixed + out_part(gathered[other], other)
    mixed = mixed + out_shift_ref[...]
    produced = (
        hidden[...].astype(jnp.float32) + layer_scale_ref[...] * mixed
    ).astype(jnp.bfloat16)
    result_ref[...] = produced

    @pl.when(pipe == 0)
    def _():
        hidden[...] = produced
        for at in range(ROW_CHUNKS):
            p_copy(at).start()

    def sent(part, at):
        owner = owner_of(part)

        @pl.when((owner <= plane) & has_up)
        def _():
            w_copy(part, at, True).wait_send()

        @pl.when((owner >= plane) & has_down)
        def _():
            w_copy(part, at, False).wait_send()

    def sent_side(part, side):
        owner = owner_of(part)

        @pl.when((owner <= plane) & has_up)
        def _():
            side_copy(part, side, True).wait_send()

        @pl.when((owner >= plane) & has_down)
        def _():
            side_copy(part, side, False).wait_send()

        @pl.when(owner != plane)
        def _():
            cross_out(part, side).wait_send()

    for at in range(direct):
        for part in range(PARTS):
            sent(part, at)

    @pl.when(pipe == 0)
    def _():
        for side in range(SIDE_CHUNKS):
            for part in range(PARTS):

                @pl.when(owner_of(part) == plane)
                def _(part=part, side=side):
                    cross_in(part, side).wait_send()

    @pl.when(pipe == 1)
    def _():
        for at in range(direct, DEPTH_CHUNKS):
            for part in range(PARTS):
                sent(part, at)
        for side in range(SIDE_CHUNKS):
            for part in range(PARTS):
                sent_side(part, side)

    for at in range(ROW_CHUNKS):
        for which in range(3):
            t_copy(which, at).wait_send()
    for pair in range(pairs):
        for which, other in enumerate(others):
            c_copy(other, which, pair).wait_send()

    @pl.when(pipe == 0)
    def _():
        for at in range(ROW_CHUNKS):
            p_copy(at).wait_send()


def fused_device(
    mesh, patches, lengths, norm_gain, norm_bias, w_qkv, w_out, out_bias, scale_gain
):
    planes, groups = mesh.shape["dp"], mesh.shape["ctx"]
    micro_count, _, rows, width = patches.shape
    group = width // groups
    fits = (
        micro_count == 1
        and mesh.shape["pipe"] == 2
        and groups == 4
        and group % 128 == 0
        and 128 % (width // HEADS) == 0
        and w_qkv.shape[2] % group == 0
        and rows % (16 * ROW_CHUNKS) == 0
        and rows <= 128
    )
    if not fits:
        return per_device(
            patches, lengths, norm_gain, norm_bias, w_qkv, w_out, out_bias, scale_gain
        )
    bf16 = jnp.bfloat16
    pairs = group // 128
    vmem = pl.BlockSpec(memory_space=pltpu.VMEM)
    hbm = pl.BlockSpec(memory_space=pl.ANY)
    dma = pltpu.SemaphoreType.DMA
    result = pl.pallas_call(
        functools.partial(fused_kernel, (rows, width, planes, group)),
        out_shape=jax.ShapeDtypeStruct((rows, width), bf16),
        in_specs=[
            pl.BlockSpec(memory_space=pltpu.SMEM),
            hbm,
            hbm,
            hbm,
            hbm,
            hbm,
            hbm,
            hbm,
        ],
        out_specs=vmem,
        scratch_shapes=[
            pltpu.VMEM((1, width), jnp.float32),
            pltpu.VMEM((1, width), jnp.float32),
            pltpu.VMEM((1, width), jnp.float32),
            pltpu.VMEM((1, width), jnp.float32),
            pltpu.VMEM((PARTS, width // DEPTH_CHUNKS * SIDE_CHUNKS, group), bf16),
            pltpu.VMEM((rows, width), bf16),
            pltpu.VMEM((groups, rows, width), bf16),
            pltpu.VMEM((PARTS, width, group), bf16),
            pltpu.VMEM((width, width), bf16),
            pltpu.VMEM((groups * rows, group), bf16),
            pltpu.VMEM((groups, rows, group), bf16),
            dma((PARTS, DEPTH_CHUNKS)),
            dma((PARTS, DEPTH_CHUNKS)),
            dma((PARTS, DEPTH_CHUNKS)),
            dma((3, ROW_CHUNKS)),
            dma((3, ROW_CHUNKS)),
            dma((3, pairs)),
            dma((3, pairs)),
            dma((ROW_CHUNKS,)),
            dma((ROW_CHUNKS,)),
            dma((PARTS, SIDE_CHUNKS)),
            dma((PARTS, SIDE_CHUNKS)),
            dma((PARTS, SIDE_CHUNKS)),
            dma((PARTS, SIDE_CHUNKS)),
            dma((9,)),
        ],
        compiler_params=pltpu.CompilerParams(
            collective_id=0, has_side_effects=True, vmem_limit_bytes=62 * 1024 * 1024
        ),
    )(
        lengths,
        patches[0, 0],
        norm_gain,
        norm_bias,
        w_qkv[0],
        w_out[0],
        out_bias,
        scale_gain,
    )
    return result[None, None, None]


def solution(mesh):
    in_specs = (
        P(None, "dp", "ctx", None),
        P(None, "dp"),
        P("pipe", None),
        P("pipe", None),
        P("pipe", None, "dp"),
        P("pipe", None, None),
        P("pipe", None),
        P("pipe", None),
    )
    out_specs = P("pipe", None, "dp", "ctx", None)
    body = functools.partial(fused_device, mesh)
    return jax.shard_map(
        body, mesh=mesh, in_specs=in_specs, out_specs=out_specs, check_vma=False
    )
```

```python
import functools
import math

import jax
import jax.numpy as jnp
from jax import lax
from jax.experimental import pallas as pl
from jax.experimental.pallas import tpu as pltpu
from jax.sharding import PartitionSpec as P

HEADS = 16


epsilon = 1e-06
masked_score = -1e30


def shifted(value, axis, by):
    count = lax.axis_size(axis)
    pairs = [(i, i + by) for i in range(count) if 0 <= i + by < count]
    return lax.ppermute(value, axis, pairs)


def normalize(hidden, gain, shift):
    values = hidden.astype(jnp.float32)
    row_mean = jnp.mean(values, axis=-1, keepdims=True)
    centered = values - row_mean
    variance = jnp.mean(centered * centered, axis=-1, keepdims=True)
    return (centered * lax.rsqrt(variance + epsilon) * gain + shift).astype(jnp.bfloat16)


def per_device(patches, lengths, norm_gain, norm_bias, w_qkv, w_out, out_bias, scale_gain):
    section_index = lax.axis_index("pipe")
    section_count = lax.axis_size("pipe")
    group_count = lax.axis_size("ctx")
    micro_count = patches.shape[0]
    tok_rows = patches.shape[2]
    width = patches.shape[3]
    head_count = HEADS
    head_width = width // head_count
    group_heads = head_count // group_count
    score_scale = head_width ** (-0.5)
    qkv_full = lax.all_gather(w_qkv[0], "dp", axis=1, tiled=True)
    out_full = w_out[0]
    gain = norm_gain[0]
    shift = norm_bias[0]
    out_shift = out_bias[0]
    layer_scale = scale_gain[0]
    turn_count = micro_count + section_count - 1
    received = jnp.zeros((tok_rows, width), jnp.bfloat16)
    results = jnp.zeros((micro_count, tok_rows, width), jnp.bfloat16)
    volume_lengths = lengths[:, 0]
    for turn_index in range(turn_count):
        fresh = patches[min(turn_index, micro_count - 1), 0]
        current = jnp.where(section_index == 0, fresh, received)
        offset_turn = turn_index - section_index
        slot_index = jnp.clip(offset_turn, 0, micro_count - 1)
        length = lax.dynamic_index_in_dim(volume_lengths, slot_index, keepdims=False)
        normed = normalize(current, gain, shift)
        run_projected = jnp.dot(normed, qkv_full, preferred_element_type=jnp.float32).astype(
            jnp.bfloat16
        )
        run_projected = run_projected.reshape(tok_rows, 3, head_count, head_width)
        split_heads = run_projected.reshape(tok_rows, 3, group_count, group_heads, head_width)
        block = lax.all_to_all(split_heads, "ctx", split_axis=2, concat_axis=0, tiled=True)
        queries = block[:, 0, 0]
        key_rows = block[:, 1, 0]
        value_rows = block[:, 2, 0]
        total_rows = key_rows.shape[0]
        local_heads = queries.shape[1]
        valid = jnp.arange(total_rows, dtype=jnp.int32) < length
        query_block = math.gcd(total_rows, 512)
        grouped = queries.reshape(total_rows // query_block, query_block, local_heads, head_width)

        def one_block(query_group):
            scores = (
                jnp.einsum(
                    "qhd,khd->hqk", query_group, key_rows, preferred_element_type=jnp.float32
                )
                * score_scale
            )
            scores = jnp.where(valid[None, None, :], scores, masked_score)
            top_score = jnp.max(scores, axis=-1, keepdims=True)
            weights = jnp.where(valid[None, None, :], jnp.exp(scores - top_score), 0.0)
            totals = jnp.sum(weights, axis=-1)
            context = (
                jnp.einsum(
                    "hqk,khd->qhd",
                    weights.astype(jnp.bfloat16),
                    value_rows,
                    preferred_element_type=jnp.float32,
                )
                / totals.T[:, :, None]
            )
            return context.astype(jnp.bfloat16)

        blocks_out = lax.map(one_block, grouped)
        per_head = blocks_out.reshape(total_rows, 1, local_heads, head_width)
        merged = lax.all_to_all(per_head, "ctx", split_axis=0, concat_axis=1, tiled=True)
        run_context = merged.reshape(tok_rows, head_count, head_width)
        run_context = run_context.reshape(tok_rows, width)
        mixed = jnp.dot(run_context, out_full, preferred_element_type=jnp.float32) + out_shift
        produced = (current.astype(jnp.float32) + layer_scale * mixed).astype(jnp.bfloat16)
        keep_it = (offset_turn >= 0) & (offset_turn < micro_count)
        previous = lax.dynamic_index_in_dim(results, slot_index, keepdims=False)
        results = lax.dynamic_update_index_in_dim(
            results, jnp.where(keep_it, produced, previous), slot_index, 0
        )
        if turn_index + 1 < turn_count:
            received = shifted(produced, "pipe", 1)
    return results[None, :, None]


MESH = pl.DeviceIdType.MESH
PARTS = 3
DEPTH_CHUNKS = 4
SIDE_CHUNKS = 1
ROW_CHUNKS = 2


def fused_kernel(
    sizes,
    length_ref,
    patches_ref,
    gain_hbm,
    shift_hbm,
    w_ref,
    out_w_ref,
    out_shift_hbm,
    layer_scale_hbm,
    result_ref,
    gain_ref,
    shift_ref,
    out_shift_ref,
    layer_scale_ref,
    side_weights,
    hidden,
    normed,
    weights,
    out_w,
    mine,
    gathered,
    w_recv,
    w_up,
    w_down,
    t_send,
    t_recv,
    c_send,
    c_recv,
    p_send,
    p_recv,
    b_recv,
    b_up,
    b_down,
    b_cross,
    l_sem,
):
    rows, width, planes, group = sizes
    head_width = width // HEADS
    group_blocks = w_ref.shape[1] // group
    depth = width // DEPTH_CHUNKS
    piece = rows // ROW_CHUNKS
    pairs = group // 128
    pipe = lax.axis_index("pipe")
    ctx = lax.axis_index("ctx")
    plane = lax.axis_index("dp")
    core, side = ctx % 2, ctx // 2
    near = side * 2 + (1 - core)
    across = (1 - side) * 2 + core
    diagonal = 3 - ctx
    others = (near, across, diagonal)
    has_up = plane < planes - 1
    has_down = plane > 0

    direct = DEPTH_CHUNKS - SIDE_CHUNKS
    patches_copy = pltpu.make_async_copy(patches_ref, hidden, l_sem.at[4])

    @pl.when(pipe == 0)
    def _():
        patches_copy.start()

    small_copies = [
        pltpu.make_async_copy(there, here, l_sem.at[5 + index])
        for index, (there, here) in enumerate(
            (
                (gain_hbm, gain_ref),
                (shift_hbm, shift_ref),
                (out_shift_hbm, out_shift_ref),
                (layer_scale_hbm, layer_scale_ref),
            )
        )
    ]
    for small_copy in small_copies:
        small_copy.start()
    out_w_copy = pltpu.make_async_copy(out_w_ref, out_w, l_sem.at[0])
    out_w_copy.start()

    def owner_of(part):
        return (part * 4 + ctx) // group_blocks

    def own_column(part):
        return pl.multiple_of(((part * 4 + ctx) % group_blocks) * group, group)

    for part in range(PARTS):
        own_copy = pltpu.make_async_copy(
            w_ref.at[:, pl.ds(own_column(part), group)], weights.at[part], l_sem.at[1 + part]
        )

        @pl.when(owner_of(part) == plane)
        def _(own_copy=own_copy):
            own_copy.start()

    barrier = pltpu.get_barrier_semaphore()
    pl.semaphore_signal(barrier, inc=1, device_id={"pipe": 1 - pipe}, device_id_type=MESH)
    for other in others:
        pl.semaphore_signal(barrier, inc=1, device_id={"ctx": other}, device_id_type=MESH)

    @pl.when(has_up)
    def _():
        pl.semaphore_signal(barrier, inc=1, device_id={"dp": plane + 1}, device_id_type=MESH)

    @pl.when(has_down)
    def _():
        pl.semaphore_signal(barrier, inc=1, device_id={"dp": plane - 1}, device_id_type=MESH)

    def normalize_piece(at):
        span = pl.ds(at * piece, piece)
        normed[ctx, span, :] = normalize(hidden[span, :], gain_ref[...], shift_ref[...])

    for small_copy in small_copies:
        small_copy.wait()

    @pl.when(pipe == 0)
    def _():
        patches_copy.wait()
        for at in range(ROW_CHUNKS):
            normalize_piece(at)

    for part in range(PARTS):
        own_copy = pltpu.make_async_copy(
            w_ref.at[:, pl.ds(own_column(part), group)], weights.at[part], l_sem.at[1 + part]
        )

        @pl.when(owner_of(part) == plane)
        def _(own_copy=own_copy):
            own_copy.wait()

    pl.semaphore_wait(barrier, 4 + has_up.astype(jnp.int32) + has_down.astype(jnp.int32))

    def w_copy(part, at, up):
        span = pl.ds(at * depth, depth)
        there = weights.at[part, span, :]
        return pltpu.make_async_remote_copy(
            src_ref=there,
            dst_ref=there,
            send_sem=(w_up if up else w_down).at[part, at],
            recv_sem=w_recv.at[part, at],
            device_id={"dp": plane + 1 if up else plane - 1},
            device_id_type=MESH,
        )

    def start_own(part, at):
        is_own = owner_of(part) == plane

        @pl.when(is_own & has_up)
        def _():
            w_copy(part, at, True).start()

        @pl.when(is_own & has_down)
        def _():
            w_copy(part, at, False).start()

    def relay(part, at):
        owner = owner_of(part)

        @pl.when((owner < plane) & has_up)
        def _():
            w_copy(part, at, True).wait_recv()
            w_copy(part, at, True).start()

        @pl.when((owner > plane) & has_down)
        def _():
            w_copy(part, at, False).wait_recv()
            w_copy(part, at, False).start()

    def arrive(part, at):
        owner = owner_of(part)

        @pl.when(((owner < plane) & (plane == planes - 1)) | ((owner > plane) & (plane == 0)))
        def _():
            w_copy(part, at, True).wait_recv()

    def distance(part):
        return jnp.abs(owner_of(part) - plane)

    def relay_from(away, count):
        for at in range(count):
            for part in range(PARTS):

                @pl.when(distance(part) == away)
                def _(part=part, at=at):
                    relay(part, at)

    def cross_in(part, side):
        span = pl.ds((direct + side) * depth, depth)
        return pltpu.make_async_remote_copy(
            src_ref=weights.at[part, span, :],
            dst_ref=side_weights.at[part, pl.ds(side * depth, depth), :],
            send_sem=b_cross.at[part, side],
            recv_sem=b_recv.at[part, side],
            device_id={"pipe": 1 - pipe},
            device_id_type=MESH,
        )

    def side_copy(part, side, up):
        block = side_weights.at[part, pl.ds(side * depth, depth), :]
        return pltpu.make_async_remote_copy(
            src_ref=block,
            dst_ref=block,
            send_sem=(b_up if up else b_down).at[part, side],
            recv_sem=b_recv.at[part, side],
            device_id={"dp": plane + 1 if up else plane - 1},
            device_id_type=MESH,
        )

    def cross_out(part, side):
        at = direct + side
        return pltpu.make_async_remote_copy(
            src_ref=side_weights.at[part, pl.ds(side * depth, depth), :],
            dst_ref=weights.at[part, pl.ds(at * depth, depth), :],
            send_sem=b_cross.at[part, side],
            recv_sem=w_recv.at[part, at],
            device_id={"pipe": 1 - pipe},
            device_id_type=MESH,
        )

    def relay_side(part, side):
        owner = owner_of(part)
        side_copy(part, side, True).wait_recv()

        @pl.when((owner <= plane) & has_up)
        def _():
            side_copy(part, side, True).start()

        @pl.when((owner >= plane) & has_down)
        def _():
            side_copy(part, side, False).start()

        @pl.when(owner != plane)
        def _():
            cross_out(part, side).start()

    @pl.when(pipe == 0)
    def _():
        for at in range(direct):
            for part in range(PARTS):
                if at < SIDE_CHUNKS:

                    @pl.when(owner_of(part) == plane)
                    def _(part=part, at=at):
                        cross_in(part, at).start()

                start_own(part, at)

    def t_copy(which, at):
        whose = across if which == 2 else ctx
        block = normed.at[whose, pl.ds(at * piece, piece), :]
        return pltpu.make_async_remote_copy(
            src_ref=block,
            dst_ref=block,
            send_sem=t_send.at[which, at],
            recv_sem=t_recv.at[which, at],
            device_id={"ctx": across if which == 1 else near},
            device_id_type=MESH,
        )

    def send_piece(at):
        t_copy(1, at).start()
        t_copy(0, at).start()

    def pass_pieces():
        for at in range(ROW_CHUNKS):
            t_copy(1, at).wait_recv()
            t_copy(2, at).start()

    @pl.when(pipe == 0)
    def _():
        for at in range(ROW_CHUNKS):
            send_piece(at)
        for away in range(1, planes):
            relay_from(away, direct)
            if away == 1:
                pass_pieces()
    @pl.when(pipe == 1)
    def _():
        for away in range(planes):
            for side in range(SIDE_CHUNKS):
                for part in range(PARTS):

                    @pl.when(distance(part) == away)
                    def _(part=part, side=side):
                        relay_side(part, side)

            if away < 2:
                for part in range(PARTS):
                    start_own(part, away)
        for at in range(2, DEPTH_CHUNKS):
            for part in range(PARTS):
                start_own(part, at)
        for away in range(1, planes):
            relay_from(away, DEPTH_CHUNKS)

    def p_copy(at):
        block = hidden.at[pl.ds(at * piece, piece), :]
        return pltpu.make_async_remote_copy(
            src_ref=block,
            dst_ref=block,
            send_sem=p_send.at[at],
            recv_sem=p_recv.at[at],
            device_id={"pipe": 1 - pipe},
            device_id_type=MESH,
        )

    @pl.when(pipe == 1)
    def _():
        for at in range(ROW_CHUNKS):
            p_copy(at).wait_recv()
            normalize_piece(at)
            send_piece(at)
        pass_pieces()

    for at in range(ROW_CHUNKS):
        t_copy(0, at).wait_recv()
        t_copy(2, at).wait_recv()

    for at in range(direct):
        for part in range(PARTS):
            arrive(part, at)

    @pl.when(pipe == 0)
    def _():
        for side in range(SIDE_CHUNKS):
            for part in range(PARTS):

                @pl.when(owner_of(part) != plane)
                def _(part=part, side=side):
                    cross_out(part, side).wait_recv()

    @pl.when(pipe == 1)
    def _():
        for at in range(direct, DEPTH_CHUNKS):
            for part in range(PARTS):
                arrive(part, at)

    total = 4 * rows
    tokens = normed[...].reshape(total, width)

    def project(part):
        return jnp.dot(tokens, weights[part], preferred_element_type=jnp.float32)

    queries = (project(0).astype(jnp.bfloat16) * jnp.bfloat16(head_width**-0.5)).astype(
        jnp.bfloat16
    )
    key_rows = project(1).astype(jnp.bfloat16)
    value_columns = project(2).T.astype(jnp.bfloat16)
    key_bias = jnp.where(
        lax.broadcasted_iota(jnp.int32, (total, 1), 0) < length_ref[0, 0], 0.0, masked_score
    )
    lane_head = lax.broadcasted_iota(jnp.int32, (total, 128), 1) // head_width

    def c_copy(other, which, pair):
        lanes = pl.ds(pair * 128, 128)
        return pltpu.make_async_remote_copy(
            src_ref=mine.at[pl.ds(pl.multiple_of(other * rows, rows), rows), lanes],
            dst_ref=gathered.at[ctx, :, lanes],
            send_sem=c_send.at[which, pair],
            recv_sem=c_recv.at[which, pair],
            device_id={"ctx": other},
            device_id_type=MESH,
        )

    per_pair = 128 // head_width
    for pair in range(pairs):
        pair_queries = queries[:, pair * 128 : (pair + 1) * 128]
        pair_keys = key_rows[:, pair * 128 : (pair + 1) * 128]
        columns = []
        for head in range(per_pair):
            head_queries = jnp.where(lane_head == head, pair_queries, jnp.bfloat16(0))
            scores = lax.dot_general(
                pair_keys,
                head_queries,
                (((1,), (1,)), ((), ())),
                preferred_element_type=jnp.float32,
            )
            scores = scores + key_bias
            top = jnp.max(scores, axis=0, keepdims=True)
            exps = jnp.exp(scores - top)
            totals = jnp.sum(exps, axis=0, keepdims=True)
            first = (pair * per_pair + head) * head_width
            part_sum = jnp.dot(
                value_columns[first : first + head_width, :],
                exps.astype(jnp.bfloat16),
                preferred_element_type=jnp.float32,
            )
            columns.append(part_sum / totals)
        context = jnp.concatenate(columns, axis=0).T.astype(jnp.bfloat16)
        mine[:, pair * 128 : (pair + 1) * 128] = context
        for which, other in ((1, across), (2, diagonal), (0, near)):
            c_copy(other, which, pair).start()

    own_rows = pl.ds(pl.multiple_of(ctx * rows, rows), rows)
    out_w_copy.wait()

    def out_part(block, whose):
        span = pl.ds(pl.multiple_of(whose * group, group), group)
        return jnp.dot(block, out_w[span, :], preferred_element_type=jnp.float32)

    mixed = out_part(mine[own_rows, :], ctx)
    for which, other in enumerate(others):
        for pair in range(pairs):
            c_copy(other, which, pair).wait_recv()
        mixed = mixed + out_part(gathered[other], other)
    mixed = mixed + out_shift_ref[...]
    produced = (
        hidden[...].astype(jnp.float32) + layer_scale_ref[...] * mixed
    ).astype(jnp.bfloat16)
    result_ref[...] = produced

    @pl.when(pipe == 0)
    def _():
        hidden[...] = produced
        for at in range(ROW_CHUNKS):
            p_copy(at).start()

    def sent(part, at):
        owner = owner_of(part)

        @pl.when((owner <= plane) & has_up)
        def _():
            w_copy(part, at, True).wait_send()

        @pl.when((owner >= plane) & has_down)
        def _():
            w_copy(part, at, False).wait_send()

    def sent_side(part, side):
        owner = owner_of(part)

        @pl.when((owner <= plane) & has_up)
        def _():
            side_copy(part, side, True).wait_send()

        @pl.when((owner >= plane) & has_down)
        def _():
            side_copy(part, side, False).wait_send()

        @pl.when(owner != plane)
        def _():
            cross_out(part, side).wait_send()

    for at in range(direct):
        for part in range(PARTS):
            sent(part, at)

    @pl.when(pipe == 0)
    def _():
        for side in range(SIDE_CHUNKS):
            for part in range(PARTS):

                @pl.when(owner_of(part) == plane)
                def _(part=part, side=side):
                    cross_in(part, side).wait_send()

    @pl.when(pipe == 1)
    def _():
        for at in range(direct, DEPTH_CHUNKS):
            for part in range(PARTS):
                sent(part, at)
        for side in range(SIDE_CHUNKS):
            for part in range(PARTS):
                sent_side(part, side)

    for at in range(ROW_CHUNKS):
        for which in range(3):
            t_copy(which, at).wait_send()
    for pair in range(pairs):
        for which, other in enumerate(others):
            c_copy(other, which, pair).wait_send()

    @pl.when(pipe == 0)
    def _():
        for at in range(ROW_CHUNKS):
            p_copy(at).wait_send()


def fused_device(
    mesh, patches, lengths, norm_gain, norm_bias, w_qkv, w_out, out_bias, scale_gain
):
    planes, groups = mesh.shape["dp"], mesh.shape["ctx"]
    micro_count, _, rows, width = patches.shape
    group = width // groups
    fits = (
        micro_count == 1
        and mesh.shape["pipe"] == 2
        and groups == 4
        and group % 128 == 0
        and 128 % (width // HEADS) == 0
        and w_qkv.shape[2] % group == 0
        and rows % (16 * ROW_CHUNKS) == 0
        and rows <= 128
    )
    if not fits:
        return per_device(
            patches, lengths, norm_gain, norm_bias, w_qkv, w_out, out_bias, scale_gain
        )
    bf16 = jnp.bfloat16
    pairs = group // 128
    vmem = pl.BlockSpec(memory_space=pltpu.VMEM)
    hbm = pl.BlockSpec(memory_space=pl.ANY)
    dma = pltpu.SemaphoreType.DMA
    result = pl.pallas_call(
        functools.partial(fused_kernel, (rows, width, planes, group)),
        out_shape=jax.ShapeDtypeStruct((rows, width), bf16),
        in_specs=[
            pl.BlockSpec(memory_space=pltpu.SMEM),
            hbm,
            hbm,
            hbm,
            hbm,
            hbm,
            hbm,
            hbm,
        ],
        out_specs=vmem,
        scratch_shapes=[
            pltpu.VMEM((1, width), jnp.float32),
            pltpu.VMEM((1, width), jnp.float32),
            pltpu.VMEM((1, width), jnp.float32),
            pltpu.VMEM((1, width), jnp.float32),
            pltpu.VMEM((PARTS, width // DEPTH_CHUNKS * SIDE_CHUNKS, group), bf16),
            pltpu.VMEM((rows, width), bf16),
            pltpu.VMEM((groups, rows, width), bf16),
            pltpu.VMEM((PARTS, width, group), bf16),
            pltpu.VMEM((width, width), bf16),
            pltpu.VMEM((groups * rows, group), bf16),
            pltpu.VMEM((groups, rows, group), bf16),
            dma((PARTS, DEPTH_CHUNKS)),
            dma((PARTS, DEPTH_CHUNKS)),
            dma((PARTS, DEPTH_CHUNKS)),
            dma((3, ROW_CHUNKS)),
            dma((3, ROW_CHUNKS)),
            dma((3, pairs)),
            dma((3, pairs)),
            dma((ROW_CHUNKS,)),
            dma((ROW_CHUNKS,)),
            dma((PARTS, SIDE_CHUNKS)),
            dma((PARTS, SIDE_CHUNKS)),
            dma((PARTS, SIDE_CHUNKS)),
            dma((PARTS, SIDE_CHUNKS)),
            dma((9,)),
        ],
        compiler_params=pltpu.CompilerParams(
            collective_id=0, has_side_effects=True, vmem_limit_bytes=62 * 1024 * 1024
        ),
    )(
        lengths,
        patches[0, 0],
        norm_gain,
        norm_bias,
        w_qkv[0],
        w_out[0],
        out_bias,
        scale_gain,
    )
    return result[None, None, None]


def solution(mesh):
    in_specs = (
        P(None, "dp", "ctx", None),
        P(None, "dp"),
        P("pipe", None),
        P("pipe", None),
        P("pipe", None, "dp"),
        P("pipe", None, None),
        P("pipe", None),
        P("pipe", None),
    )
    out_specs = P("pipe", None, "dp", "ctx", None)
    body = functools.partial(fused_device, mesh)
    return jax.shard_map(
        body, mesh=mesh, in_specs=in_specs, out_specs=out_specs, check_vma=False
    )
```

```python
import functools
import math

import jax
import jax.numpy as jnp
from jax import lax
from jax.experimental import pallas as pl
from jax.experimental.pallas import tpu as pltpu
from jax.sharding import PartitionSpec as P

HEADS = 16


epsilon = 1e-06
masked_score = -1e30


def shifted(value, axis, by):
    count = lax.axis_size(axis)
    pairs = [(i, i + by) for i in range(count) if 0 <= i + by < count]
    return lax.ppermute(value, axis, pairs)


def normalize(hidden, gain, shift):
    values = hidden.astype(jnp.float32)
    row_mean = jnp.mean(values, axis=-1, keepdims=True)
    centered = values - row_mean
    variance = jnp.mean(centered * centered, axis=-1, keepdims=True)
    return (centered * lax.rsqrt(variance + epsilon) * gain + shift).astype(jnp.bfloat16)


def per_device(patches, lengths, norm_gain, norm_bias, w_qkv, w_out, out_bias, scale_gain):
    section_index = lax.axis_index("pipe")
    section_count = lax.axis_size("pipe")
    group_count = lax.axis_size("ctx")
    micro_count = patches.shape[0]
    tok_rows = patches.shape[2]
    width = patches.shape[3]
    head_count = HEADS
    head_width = width // head_count
    group_heads = head_count // group_count
    score_scale = head_width ** (-0.5)
    qkv_full = lax.all_gather(w_qkv[0], "dp", axis=1, tiled=True)
    out_full = w_out[0]
    gain = norm_gain[0]
    shift = norm_bias[0]
    out_shift = out_bias[0]
    layer_scale = scale_gain[0]
    turn_count = micro_count + section_count - 1
    received = jnp.zeros((tok_rows, width), jnp.bfloat16)
    results = jnp.zeros((micro_count, tok_rows, width), jnp.bfloat16)
    volume_lengths = lengths[:, 0]
    for turn_index in range(turn_count):
        fresh = patches[min(turn_index, micro_count - 1), 0]
        current = jnp.where(section_index == 0, fresh, received)
        offset_turn = turn_index - section_index
        slot_index = jnp.clip(offset_turn, 0, micro_count - 1)
        length = lax.dynamic_index_in_dim(volume_lengths, slot_index, keepdims=False)
        normed = normalize(current, gain, shift)
        run_projected = jnp.dot(normed, qkv_full, preferred_element_type=jnp.float32).astype(
            jnp.bfloat16
        )
        run_projected = run_projected.reshape(tok_rows, 3, head_count, head_width)
        split_heads = run_projected.reshape(tok_rows, 3, group_count, group_heads, head_width)
        block = lax.all_to_all(split_heads, "ctx", split_axis=2, concat_axis=0, tiled=True)
        queries = block[:, 0, 0]
        key_rows = block[:, 1, 0]
        value_rows = block[:, 2, 0]
        total_rows = key_rows.shape[0]
        local_heads = queries.shape[1]
        valid = jnp.arange(total_rows, dtype=jnp.int32) < length
        query_block = math.gcd(total_rows, 512)
        grouped = queries.reshape(total_rows // query_block, query_block, local_heads, head_width)

        def one_block(query_group):
            scores = (
                jnp.einsum(
                    "qhd,khd->hqk", query_group, key_rows, preferred_element_type=jnp.float32
                )
                * score_scale
            )
            scores = jnp.where(valid[None, None, :], scores, masked_score)
            top_score = jnp.max(scores, axis=-1, keepdims=True)
            weights = jnp.where(valid[None, None, :], jnp.exp(scores - top_score), 0.0)
            totals = jnp.sum(weights, axis=-1)
            context = (
                jnp.einsum(
                    "hqk,khd->qhd",
                    weights.astype(jnp.bfloat16),
                    value_rows,
                    preferred_element_type=jnp.float32,
                )
                / totals.T[:, :, None]
            )
            return context.astype(jnp.bfloat16)

        blocks_out = lax.map(one_block, grouped)
        per_head = blocks_out.reshape(total_rows, 1, local_heads, head_width)
        merged = lax.all_to_all(per_head, "ctx", split_axis=0, concat_axis=1, tiled=True)
        run_context = merged.reshape(tok_rows, head_count, head_width)
        run_context = run_context.reshape(tok_rows, width)
        mixed = jnp.dot(run_context, out_full, preferred_element_type=jnp.float32) + out_shift
        produced = (current.astype(jnp.float32) + layer_scale * mixed).astype(jnp.bfloat16)
        keep_it = (offset_turn >= 0) & (offset_turn < micro_count)
        previous = lax.dynamic_index_in_dim(results, slot_index, keepdims=False)
        results = lax.dynamic_update_index_in_dim(
            results, jnp.where(keep_it, produced, previous), slot_index, 0
        )
        if turn_index + 1 < turn_count:
            received = shifted(produced, "pipe", 1)
    return results[None, :, None]


MESH = pl.DeviceIdType.MESH
PARTS = 3
DEPTH_CHUNKS = 4
SIDE_CHUNKS = 1
ROW_CHUNKS = 4


def fused_kernel(
    sizes,
    length_ref,
    patches_ref,
    gain_hbm,
    shift_hbm,
    w_ref,
    out_w_ref,
    out_shift_hbm,
    layer_scale_hbm,
    result_ref,
    gain_ref,
    shift_ref,
    out_shift_ref,
    layer_scale_ref,
    side_weights,
    hidden,
    normed,
    weights,
    out_w,
    mine,
    gathered,
    w_recv,
    w_up,
    w_down,
    t_send,
    t_recv,
    c_send,
    c_recv,
    p_send,
    p_recv,
    b_recv,
    b_up,
    b_down,
    b_cross,
    l_sem,
):
    rows, width, planes, group = sizes
    head_width = width // HEADS
    group_blocks = w_ref.shape[1] // group
    depth = width // DEPTH_CHUNKS
    piece = rows // ROW_CHUNKS
    pairs = group // 128
    pipe = lax.axis_index("pipe")
    ctx = lax.axis_index("ctx")
    plane = lax.axis_index("dp")
    core, side = ctx % 2, ctx // 2
    near = side * 2 + (1 - core)
    across = (1 - side) * 2 + core
    diagonal = 3 - ctx
    others = (near, across, diagonal)
    has_up = plane < planes - 1
    has_down = plane > 0

    direct = DEPTH_CHUNKS - SIDE_CHUNKS
    patches_copy = pltpu.make_async_copy(patches_ref, hidden, l_sem.at[4])

    @pl.when(pipe == 0)
    def _():
        patches_copy.start()

    small_copies = [
        pltpu.make_async_copy(there, here, l_sem.at[5 + index])
        for index, (there, here) in enumerate(
            (
                (gain_hbm, gain_ref),
                (shift_hbm, shift_ref),
                (out_shift_hbm, out_shift_ref),
                (layer_scale_hbm, layer_scale_ref),
            )
        )
    ]
    for small_copy in small_copies:
        small_copy.start()
    out_w_copy = pltpu.make_async_copy(out_w_ref, out_w, l_sem.at[0])
    out_w_copy.start()

    def owner_of(part):
        return (part * 4 + ctx) // group_blocks

    def own_column(part):
        return pl.multiple_of(((part * 4 + ctx) % group_blocks) * group, group)

    for part in range(PARTS):
        own_copy = pltpu.make_async_copy(
            w_ref.at[:, pl.ds(own_column(part), group)], weights.at[part], l_sem.at[1 + part]
        )

        @pl.when(owner_of(part) == plane)
        def _(own_copy=own_copy):
            own_copy.start()

    barrier = pltpu.get_barrier_semaphore()
    pl.semaphore_signal(barrier, inc=1, device_id={"pipe": 1 - pipe}, device_id_type=MESH)
    for other in others:
        pl.semaphore_signal(barrier, inc=1, device_id={"ctx": other}, device_id_type=MESH)

    @pl.when(has_up)
    def _():
        pl.semaphore_signal(barrier, inc=1, device_id={"dp": plane + 1}, device_id_type=MESH)

    @pl.when(has_down)
    def _():
        pl.semaphore_signal(barrier, inc=1, device_id={"dp": plane - 1}, device_id_type=MESH)

    def normalize_piece(at):
        span = pl.ds(at * piece, piece)
        normed[ctx, span, :] = normalize(hidden[span, :], gain_ref[...], shift_ref[...])

    for small_copy in small_copies:
        small_copy.wait()

    @pl.when(pipe == 0)
    def _():
        patches_copy.wait()
        for at in range(ROW_CHUNKS):
            normalize_piece(at)

    for part in range(PARTS):
        own_copy = pltpu.make_async_copy(
            w_ref.at[:, pl.ds(own_column(part), group)], weights.at[part], l_sem.at[1 + part]
        )

        @pl.when(owner_of(part) == plane)
        def _(own_copy=own_copy):
            own_copy.wait()

    pl.semaphore_wait(barrier, 4 + has_up.astype(jnp.int32) + has_down.astype(jnp.int32))

    def w_copy(part, at, up):
        span = pl.ds(at * depth, depth)
        there = weights.at[part, span, :]
        return pltpu.make_async_remote_copy(
            src_ref=there,
            dst_ref=there,
            send_sem=(w_up if up else w_down).at[part, at],
            recv_sem=w_recv.at[part, at],
            device_id={"dp": plane + 1 if up else plane - 1},
            device_id_type=MESH,
        )

    def start_own(part, at):
        is_own = owner_of(part) == plane

        @pl.when(is_own & has_up)
        def _():
            w_copy(part, at, True).start()

        @pl.when(is_own & has_down)
        def _():
            w_copy(part, at, False).start()

    def relay(part, at):
        owner = owner_of(part)

        @pl.when((owner < plane) & has_up)
        def _():
            w_copy(part, at, True).wait_recv()
            w_copy(part, at, True).start()

        @pl.when((owner > plane) & has_down)
        def _():
            w_copy(part, at, False).wait_recv()
            w_copy(part, at, False).start()

    def arrive(part, at):
        owner = owner_of(part)

        @pl.when(((owner < plane) & (plane == planes - 1)) | ((owner > plane) & (plane == 0)))
        def _():
            w_copy(part, at, True).wait_recv()

    def distance(part):
        return jnp.abs(owner_of(part) - plane)

    def relay_from(away, count):
        for at in range(count):
            for part in range(PARTS):

                @pl.when(distance(part) == away)
                def _(part=part, at=at):
                    relay(part, at)

    def cross_in(part, side):
        span = pl.ds((direct + side) * depth, depth)
        return pltpu.make_async_remote_copy(
            src_ref=weights.at[part, span, :],
            dst_ref=side_weights.at[part, pl.ds(side * depth, depth), :],
            send_sem=b_cross.at[part, side],
            recv_sem=b_recv.at[part, side],
            device_id={"pipe": 1 - pipe},
            device_id_type=MESH,
        )

    def side_copy(part, side, up):
        block = side_weights.at[part, pl.ds(side * depth, depth), :]
        return pltpu.make_async_remote_copy(
            src_ref=block,
            dst_ref=block,
            send_sem=(b_up if up else b_down).at[part, side],
            recv_sem=b_recv.at[part, side],
            device_id={"dp": plane + 1 if up else plane - 1},
            device_id_type=MESH,
        )

    def cross_out(part, side):
        at = direct + side
        return pltpu.make_async_remote_copy(
            src_ref=side_weights.at[part, pl.ds(side * depth, depth), :],
            dst_ref=weights.at[part, pl.ds(at * depth, depth), :],
            send_sem=b_cross.at[part, side],
            recv_sem=w_recv.at[part, at],
            device_id={"pipe": 1 - pipe},
            device_id_type=MESH,
        )

    def relay_side(part, side):
        owner = owner_of(part)
        side_copy(part, side, True).wait_recv()

        @pl.when((owner <= plane) & has_up)
        def _():
            side_copy(part, side, True).start()

        @pl.when((owner >= plane) & has_down)
        def _():
            side_copy(part, side, False).start()

        @pl.when(owner != plane)
        def _():
            cross_out(part, side).start()

    @pl.when(pipe == 0)
    def _():
        for at in range(direct):
            for part in range(PARTS):
                if at < SIDE_CHUNKS:

                    @pl.when(owner_of(part) == plane)
                    def _(part=part, at=at):
                        cross_in(part, at).start()

                start_own(part, at)

    def t_copy(which, at):
        whose = across if which == 2 else ctx
        block = normed.at[whose, pl.ds(at * piece, piece), :]
        return pltpu.make_async_remote_copy(
            src_ref=block,
            dst_ref=block,
            send_sem=t_send.at[which, at],
            recv_sem=t_recv.at[which, at],
            device_id={"ctx": across if which == 1 else near},
            device_id_type=MESH,
        )

    def send_piece(at):
        t_copy(1, at).start()
        t_copy(0, at).start()

    def pass_pieces():
        for at in range(ROW_CHUNKS):
            t_copy(1, at).wait_recv()
            t_copy(2, at).start()

    @pl.when(pipe == 0)
    def _():
        for at in range(ROW_CHUNKS):
            send_piece(at)
        for away in range(1, planes):
            relay_from(away, direct)
            if away == 1:
                pass_pieces()
    @pl.when(pipe == 1)
    def _():
        for away in range(planes):
            for side in range(SIDE_CHUNKS):
                for part in range(PARTS):

                    @pl.when(distance(part) == away)
                    def _(part=part, side=side):
                        relay_side(part, side)

            if away < 2:
                for part in range(PARTS):
                    start_own(part, away)
        for at in range(2, DEPTH_CHUNKS):
            for part in range(PARTS):
                start_own(part, at)
        for away in range(1, planes):
            relay_from(away, DEPTH_CHUNKS)

    def p_copy(at):
        block = hidden.at[pl.ds(at * piece, piece), :]
        return pltpu.make_async_remote_copy(
            src_ref=block,
            dst_ref=block,
            send_sem=p_send.at[at],
            recv_sem=p_recv.at[at],
            device_id={"pipe": 1 - pipe},
            device_id_type=MESH,
        )

    @pl.when(pipe == 1)
    def _():
        for at in range(ROW_CHUNKS):
            p_copy(at).wait_recv()
            normalize_piece(at)
            send_piece(at)
        pass_pieces()

    for at in range(ROW_CHUNKS):
        t_copy(0, at).wait_recv()
        t_copy(2, at).wait_recv()

    for at in range(direct):
        for part in range(PARTS):
            arrive(part, at)

    @pl.when(pipe == 0)
    def _():
        for side in range(SIDE_CHUNKS):
            for part in range(PARTS):

                @pl.when(owner_of(part) != plane)
                def _(part=part, side=side):
                    cross_out(part, side).wait_recv()

    @pl.when(pipe == 1)
    def _():
        for at in range(direct, DEPTH_CHUNKS):
            for part in range(PARTS):
                arrive(part, at)

    total = 4 * rows
    tokens = normed[...].reshape(total, width)

    def project(part):
        return jnp.dot(tokens, weights[part], preferred_element_type=jnp.float32)

    queries = (project(0).astype(jnp.bfloat16) * jnp.bfloat16(head_width**-0.5)).astype(
        jnp.bfloat16
    )
    key_rows = project(1).astype(jnp.bfloat16)
    value_columns = project(2).T.astype(jnp.bfloat16)
    key_bias = jnp.where(
        lax.broadcasted_iota(jnp.int32, (total, 1), 0) < length_ref[0, 0], 0.0, masked_score
    )
    lane_head = lax.broadcasted_iota(jnp.int32, (total, 128), 1) // head_width

    def c_copy(other, which, pair):
        lanes = pl.ds(pair * 128, 128)
        return pltpu.make_async_remote_copy(
            src_ref=mine.at[pl.ds(pl.multiple_of(other * rows, rows), rows), lanes],
            dst_ref=gathered.at[ctx, :, lanes],
            send_sem=c_send.at[which, pair],
            recv_sem=c_recv.at[which, pair],
            device_id={"ctx": other},
            device_id_type=MESH,
        )

    per_pair = 128 // head_width
    for pair in range(pairs):
        pair_queries = queries[:, pair * 128 : (pair + 1) * 128]
        pair_keys = key_rows[:, pair * 128 : (pair + 1) * 128]
        columns = []
        for head in range(per_pair):
            head_queries = jnp.where(lane_head == head, pair_queries, jnp.bfloat16(0))
            scores = lax.dot_general(
                pair_keys,
                head_queries,
                (((1,), (1,)), ((), ())),
                preferred_element_type=jnp.float32,
            )
            scores = scores + key_bias
            top = jnp.max(scores, axis=0, keepdims=True)
            exps = jnp.exp(scores - top)
            totals = jnp.sum(exps, axis=0, keepdims=True)
            first = (pair * per_pair + head) * head_width
            part_sum = jnp.dot(
                value_columns[first : first + head_width, :],
                exps.astype(jnp.bfloat16),
                preferred_element_type=jnp.float32,
            )
            columns.append(part_sum / totals)
        context = jnp.concatenate(columns, axis=0).T.astype(jnp.bfloat16)
        mine[:, pair * 128 : (pair + 1) * 128] = context
        for which, other in ((1, across), (2, diagonal), (0, near)):
            c_copy(other, which, pair).start()

    own_rows = pl.ds(pl.multiple_of(ctx * rows, rows), rows)
    out_w_copy.wait()

    def out_part(block, whose):
        span = pl.ds(pl.multiple_of(whose * group, group), group)
        return jnp.dot(block, out_w[span, :], preferred_element_type=jnp.float32)

    mixed = out_part(mine[own_rows, :], ctx)
    for which, other in enumerate(others):
        for pair in range(pairs):
            c_copy(other, which, pair).wait_recv()
        mixed = mixed + out_part(gathered[other], other)
    mixed = mixed + out_shift_ref[...]
    produced = (
        hidden[...].astype(jnp.float32) + layer_scale_ref[...] * mixed
    ).astype(jnp.bfloat16)
    result_ref[...] = produced

    @pl.when(pipe == 0)
    def _():
        hidden[...] = produced
        for at in range(ROW_CHUNKS):
            p_copy(at).start()

    def sent(part, at):
        owner = owner_of(part)

        @pl.when((owner <= plane) & has_up)
        def _():
            w_copy(part, at, True).wait_send()

        @pl.when((owner >= plane) & has_down)
        def _():
            w_copy(part, at, False).wait_send()

    def sent_side(part, side):
        owner = owner_of(part)

        @pl.when((owner <= plane) & has_up)
        def _():
            side_copy(part, side, True).wait_send()

        @pl.when((owner >= plane) & has_down)
        def _():
            side_copy(part, side, False).wait_send()

        @pl.when(owner != plane)
        def _():
            cross_out(part, side).wait_send()

    for at in range(direct):
        for part in range(PARTS):
            sent(part, at)

    @pl.when(pipe == 0)
    def _():
        for side in range(SIDE_CHUNKS):
            for part in range(PARTS):

                @pl.when(owner_of(part) == plane)
                def _(part=part, side=side):
                    cross_in(part, side).wait_send()

    @pl.when(pipe == 1)
    def _():
        for at in range(direct, DEPTH_CHUNKS):
            for part in range(PARTS):
                sent(part, at)
        for side in range(SIDE_CHUNKS):
            for part in range(PARTS):
                sent_side(part, side)

    for at in range(ROW_CHUNKS):
        for which in range(3):
            t_copy(which, at).wait_send()
    for pair in range(pairs):
        for which, other in enumerate(others):
            c_copy(other, which, pair).wait_send()

    @pl.when(pipe == 0)
    def _():
        for at in range(ROW_CHUNKS):
            p_copy(at).wait_send()


def fused_device(
    mesh, patches, lengths, norm_gain, norm_bias, w_qkv, w_out, out_bias, scale_gain
):
    planes, groups = mesh.shape["dp"], mesh.shape["ctx"]
    micro_count, _, rows, width = patches.shape
    group = width // groups
    fits = (
        micro_count == 1
        and mesh.shape["pipe"] == 2
        and groups == 4
        and group % 128 == 0
        and 128 % (width // HEADS) == 0
        and w_qkv.shape[2] % group == 0
        and rows % (16 * ROW_CHUNKS) == 0
        and rows <= 128
    )
    if not fits:
        return per_device(
            patches, lengths, norm_gain, norm_bias, w_qkv, w_out, out_bias, scale_gain
        )
    bf16 = jnp.bfloat16
    pairs = group // 128
    vmem = pl.BlockSpec(memory_space=pltpu.VMEM)
    hbm = pl.BlockSpec(memory_space=pl.ANY)
    dma = pltpu.SemaphoreType.DMA
    result = pl.pallas_call(
        functools.partial(fused_kernel, (rows, width, planes, group)),
        out_shape=jax.ShapeDtypeStruct((rows, width), bf16),
        in_specs=[
            pl.BlockSpec(memory_space=pltpu.SMEM),
            hbm,
            hbm,
            hbm,
            hbm,
            hbm,
            hbm,
            hbm,
        ],
        out_specs=vmem,
        scratch_shapes=[
            pltpu.VMEM((1, width), jnp.float32),
            pltpu.VMEM((1, width), jnp.float32),
            pltpu.VMEM((1, width), jnp.float32),
            pltpu.VMEM((1, width), jnp.float32),
            pltpu.VMEM((PARTS, width // DEPTH_CHUNKS * SIDE_CHUNKS, group), bf16),
            pltpu.VMEM((rows, width), bf16),
            pltpu.VMEM((groups, rows, width), bf16),
            pltpu.VMEM((PARTS, width, group), bf16),
            pltpu.VMEM((width, width), bf16),
            pltpu.VMEM((groups * rows, group), bf16),
            pltpu.VMEM((groups, rows, group), bf16),
            dma((PARTS, DEPTH_CHUNKS)),
            dma((PARTS, DEPTH_CHUNKS)),
            dma((PARTS, DEPTH_CHUNKS)),
            dma((3, ROW_CHUNKS)),
            dma((3, ROW_CHUNKS)),
            dma((3, pairs)),
            dma((3, pairs)),
            dma((ROW_CHUNKS,)),
            dma((ROW_CHUNKS,)),
            dma((PARTS, SIDE_CHUNKS)),
            dma((PARTS, SIDE_CHUNKS)),
            dma((PARTS, SIDE_CHUNKS)),
            dma((PARTS, SIDE_CHUNKS)),
            dma((9,)),
        ],
        compiler_params=pltpu.CompilerParams(
            collective_id=0, has_side_effects=True, vmem_limit_bytes=62 * 1024 * 1024
        ),
    )(
        lengths,
        patches[0, 0],
        norm_gain,
        norm_bias,
        w_qkv[0],
        w_out[0],
        out_bias,
        scale_gain,
    )
    return result[None, None, None]


def solution(mesh):
    in_specs = (
        P(None, "dp", "ctx", None),
        P(None, "dp"),
        P("pipe", None),
        P("pipe", None),
        P("pipe", None, "dp"),
        P("pipe", None, None),
        P("pipe", None),
        P("pipe", None),
    )
    out_specs = P("pipe", None, "dp", "ctx", None)
    body = functools.partial(fused_device, mesh)
    return jax.shard_map(
        body, mesh=mesh, in_specs=in_specs, out_specs=out_specs, check_vma=False
    )
```
